128 devices in a mesh: cfg: 2 (over z_hi), blk: 16 (over z_lo, x, core), ulysses: 4 (over y).
Axes of the slice: x: 4, y: 4, z: 4 (z_hi: 2, z_lo: 2; z = z_hi * 2 + z_lo), core: 2. Of those that a mesh axis runs over, the one named last changes fastest.
Arguments:
- latents: bfloat16 [8192, 3072], P(('blk', 'ulysses')), may hold values from -6 to 6
- w_qkv: bfloat16 [3072, 3, 3072], P(None, None, 'ulysses'), may hold values from -0.109375 to 0.109375
- w_out: bfloat16 [3072, 3072], P('ulysses'), may hold values from -0.109375 to 0.109375
- q_gain: float32 [128], replicated, may hold values from 1 to 3
- k_gain: float32 [128], replicated, may hold values from 1 to 3
- text_kv: bfloat16 [2, 2, 256, 3072], P(None, None, None, 'ulysses'), may hold values from -1000 to 1000, as said below
- text_lengths: int32 [2], replicated, may hold values from 64 to 256
- sigmas: float32 [51], replicated, may hold values from 0.02 to 1
- step_index: int32 [1], replicated, may hold values from 0 to 49
- guidance: float32 [1], replicated, may hold values from 4 to 8
Outputs:
- guided_velocity: bfloat16 [8192, 3072], P(('blk', 'ulysses'), 'cfg')
- next_latents: bfloat16 [8192, 3072], P(('blk', 'ulysses'), 'cfg')
The draws below stay inside these ranges and needn't reach their ends.
Inputs may be any that keep to these rules, and one draw needn't show every extreme that they name: `text_kv`: text keys and values of both prompts.
All inputs are finite; a program needn't handle non-finite values.
Results may differ from the reference program's by a relative error of at most 0.019.
Values may be sent and summed in bfloat16 or wider, within the bound.
A program may use at most 128 MiB of HBM per device.

```python
import math
import jax
import jax.numpy as jnp
from jax import lax

D = 3072
HEADS = 24
HD = 128
TXT = 256
STEPS = 1
NSIG = 51
VIDEO = 8192


def draw_text_kv(key, part):
    key = jax.random.fold_in(key, 11)
    base_key, value_key = jax.random.split(key, 2)
    keys_drawn = jnp.clip(jax.random.normal(base_key, (2, TXT, D), jnp.float32), -8.0, 8.0) * 3.5
    values_drawn = jnp.clip(jax.random.normal(value_key, (2, TXT, D), jnp.float32), -6.0, 6.0)
    return jnp.stack([keys_drawn, values_drawn], axis=1).astype(jnp.bfloat16)


def level_of(key, shape, pieces, smallest, largest):
    factor_of = 1.0
    for dim, shards_of in pieces:
        steps = jax.random.uniform(jax.random.fold_in(jax.random.fold_in(key, 6), dim), (shards_of,), jnp.float32, smallest / len(pieces), largest / len(pieces))
        factor_of = factor_of * jnp.repeat(jnp.exp(steps), shape[dim] // shards_of).reshape((-1,) + (1,) * (len(shape) - 1 - dim))
    return factor_of


def bell_draw(own_key, dims, spread, most, cuts=(), dtype=jnp.bfloat16):
    array = spread * jax.random.normal(own_key, dims, jnp.float32)
    if cuts:
        array = array * level_of(own_key, dims, cuts, -0.22, 0.18)
    return jnp.clip(array, -most, most).astype(dtype)


def setup_inputs(seed: int = 0) -> dict:
    arg_keys = jax.random.split(jax.random.key(seed), 11)
    return {
        "latents": bell_draw(arg_keys[0], (VIDEO, D), 1.0, 6.0, ((0, 64),)),
        "w_qkv": bell_draw(arg_keys[1], (D, 3, D), D ** -0.5, 0.109375, ((2, 4),)),
        "w_out": bell_draw(arg_keys[2], (D, D), D ** -0.5, 0.109375, ((0, 4),)),
        "q_gain": jnp.clip(jnp.exp(jax.random.uniform(arg_keys[3], (HD,), jnp.float32, math.log(1.0), math.log(3.0))), 1.0, 3.0),
        "k_gain": jnp.clip(jnp.exp(jax.random.uniform(arg_keys[4], (HD,), jnp.float32, math.log(1.0), math.log(3.0))), 1.0, 3.0),
        "text_kv": draw_text_kv(jax.random.fold_in(arg_keys[10], 71), 0),
        "text_lengths": jax.random.randint(arg_keys[6], (2,), TXT // 4, TXT + 1).astype(jnp.int32),
        "sigmas": jnp.clip(jnp.exp(jax.random.uniform(arg_keys[7], (NSIG,), jnp.float32, math.log(0.02), math.log(1.0))), 0.02, 1.0),
        "step_index": jax.random.randint(arg_keys[8], (STEPS,), 0, NSIG - 1).astype(jnp.int32),
        "guidance": jnp.clip(jax.random.uniform(arg_keys[9], (1,), jnp.float32, 4.0, 8.0), 4.0, 8.0),
    }


epsilon = 1e-06

def head_norm(values, gain_vector):
    shaped = values.reshape(values.shape[0], -1, HD)
    mean_square = lax.optimization_barrier(jnp.mean(shaped * shaped, axis=-1, keepdims=True))
    return (shaped * lax.rsqrt(mean_square + epsilon) * gain_vector).astype(jnp.bfloat16)

def through_bf16(values):
    return lax.optimization_barrier(values.astype(jnp.bfloat16)).astype(jnp.float32)

def attend_head(head_inputs, text_lengths):
    query_head, key_head, value_head, text_keys, text_values = head_inputs
    block_rows = 512 if VIDEO % 512 == 0 else VIDEO
    scale_factor = 1.0 / math.sqrt(HD)
    text_valid = jnp.arange(TXT)[None, :] < text_lengths[:, None]

    def one_block(query_block):
        video_scores = jnp.dot(query_block, key_head.T, preferred_element_type=jnp.float32) * scale_factor
        outputs = []
        for half_number in range(2):
            text_scores = jnp.dot(query_block, text_keys[half_number].T, preferred_element_type=jnp.float32) * scale_factor
            text_scores = jnp.where(text_valid[half_number][None, :], text_scores, -jnp.inf)
            row_max = jnp.maximum(lax.optimization_barrier(jnp.max(video_scores, axis=1)), lax.optimization_barrier(jnp.max(text_scores, axis=1)))[:, None]
            video_weights = jnp.exp(video_scores - row_max)
            text_weights = jnp.exp(text_scores - row_max)
            weight_sum = lax.optimization_barrier(jnp.sum(video_weights, axis=1)) + lax.optimization_barrier(jnp.sum(text_weights, axis=1))
            weighted = jnp.dot(video_weights.astype(jnp.bfloat16), value_head, preferred_element_type=jnp.float32)
            weighted = weighted + jnp.dot(text_weights.astype(jnp.bfloat16), text_values[half_number], preferred_element_type=jnp.float32)
            outputs.append(weighted / weight_sum[:, None])
        return jnp.stack(outputs)
    blocks = query_head.reshape(VIDEO // block_rows, block_rows, HD)
    result = lax.map(one_block, blocks)
    return jnp.transpose(result, (1, 0, 2, 3)).reshape(2, VIDEO, HD)

def reference(latents, w_qkv, w_out, q_gain, k_gain, text_kv, text_lengths, sigmas, step_index, guidance):
    latent_now = latents
    guided = jnp.zeros((VIDEO, D), jnp.float32)
    text_heads = text_kv.reshape(2, 2, TXT, HEADS, HD)
    text_keys = jnp.transpose(text_heads[:, 0], (2, 0, 1, 3))
    text_values = jnp.transpose(text_heads[:, 1], (2, 0, 1, 3))
    for step_number in range(STEPS):
        projected = jnp.dot(latent_now, w_qkv.reshape(D, 3 * D), preferred_element_type=jnp.float32).reshape(VIDEO, 3, D)
        queries = head_norm(projected[:, 0], q_gain)
        keys_all = head_norm(projected[:, 1], k_gain)
        values_all = projected[:, 2].astype(jnp.bfloat16).reshape(VIDEO, HEADS, HD)
        head_inputs = (jnp.transpose(queries, (1, 0, 2)), jnp.transpose(keys_all, (1, 0, 2)), jnp.transpose(values_all, (1, 0, 2)), text_keys, text_values)
        per_head = lax.map(lambda inputs: attend_head(inputs, text_lengths), head_inputs)
        attention = jnp.transpose(per_head, (1, 2, 0, 3)).reshape(2, VIDEO, D).astype(jnp.bfloat16)
        cond_velocity = through_bf16(jnp.dot(attention[0], w_out, preferred_element_type=jnp.float32))
        uncond_velocity = through_bf16(jnp.dot(attention[1], w_out, preferred_element_type=jnp.float32))
        guided = uncond_velocity + guidance[0] * (cond_velocity - uncond_velocity)
        position = step_index[step_number]
        sigma_step = sigmas[position + 1] - sigmas[position]
        latent_now = (latent_now.astype(jnp.float32) + sigma_step * guided).astype(jnp.bfloat16)
    return (guided.astype(jnp.bfloat16), latent_now)
```

```python
import functools
import math

import jax
import jax.numpy as jnp
from jax import lax
from jax.experimental import pallas as pl
from jax.experimental.pallas import tpu as pltpu
from jax.sharding import PartitionSpec as P

HD = 128
EPS = 1e-06
LOG2E = math.log2(math.e)
SCORE = LOG2E / math.sqrt(HD)
MESH = pl.DeviceIdType.MESH
NT = (((1,), (1,)), ((), ()))
TN = (((0,), (0,)), ((), ()))
F32 = jnp.float32
BF16 = jnp.bfloat16

HEADS = 3
ROWS = 64
GROUP = 8 * ROWS
WIDTH = 3072
HALF = WIDTH // 2
OWN = HEADS * HD
KEY_CHUNK = 256
OUT_CHUNK = 768
MESSAGES = 128


def place():
    blk = lax.axis_index("blk")
    z_hi = lax.axis_index("cfg")
    core = lax.rem(blk, 2)
    x = lax.rem(lax.div(blk, 2), 4)
    z = z_hi * 2 + lax.div(blk, 8)
    return x, lax.axis_index("ulysses"), z, core, z_hi


def step_kernel(
    x_hbm,
    wqkv_hbm,
    wout_hbm,
    text_hbm,
    qgain_ref,
    kgain_ref,
    lengths_ref,
    sigmas_ref,
    index_ref,
    guidance_ref,
    guided_ref,
    next_ref,
    xg,
    wq,
    wo,
    text,
    xcols,
    qbuf,
    kbuf,
    vbuf,
    qtext,
    textout,
    textstat,
    osend,
    orecv,
    lsend,
    lrecv,
    oown,
    lown,
    asend,
    abuf,
    dsend,
    drecv,
    nsend,
    nrecv,
    pown,
    csend,
    crecv,
    local_sem,
    send_sem,
    recv_sem,
):
    x, y, z, core, z_hi = place()

    def device(dx, dy, dz, dc):
        tx = lax.rem(x + dx + 4, 4)
        ty = lax.rem(y + dy + 4, 4)
        tz = lax.rem(z + dz + 4, 4)
        tc = lax.rem(core + dc, 2)
        return (lax.div(tz, 2), lax.rem(tz, 2) * 8 + tx * 2 + tc, ty)

    def key_device(d):
        return device((1 - core) * d, 0, core * d, 0)

    def query_device(d):
        return device(core * d, 0, (1 - core) * d, 0)

    locals_started = []

    def local(src, dst):
        copy = pltpu.make_async_copy(src, dst, local_sem.at[len(locals_started)])
        copy.start()
        locals_started.append(copy)
        return copy

    own_rows = x_hbm.at[pl.ds(pl.multiple_of(z_hi * ROWS, ROWS), ROWS)]
    own_copy = local(own_rows, xg.at[0, 0])
    own_col = core * OWN
    w_copies = []
    order = [(1, 0), (2, 0), (0, 0), (1, 1), (2, 1), (0, 1), (1, 2), (2, 2), (0, 2)]
    for place_at, (which, head) in enumerate(order):
        w_copies.append(
            local(
                wqkv_hbm.at[which, :, pl.ds(pl.multiple_of(own_col + head * HD, HD), HD)],
                wq.at[:, pl.ds(place_at * HD, HD)],
            )
        )
    text_copy = local(text_hbm.at[:, :, :, pl.ds(pl.multiple_of(own_col, HD), OWN)], text)
    wo_copies = []
    for rel_row in range(2):
        row_at = (core if rel_row == 0 else 1 - core) * OWN
        for rel_col in range(2):
            col_at = (1 - z_hi if rel_col == 0 else z_hi) * HALF
            wo_copies.append(
                local(
                    wout_hbm.at[
                        pl.ds(pl.multiple_of(row_at, OWN), OWN),
                        pl.ds(pl.multiple_of(col_at, HALF), HALF),
                    ],
                    wo.at[pl.ds(rel_row * OWN, OWN), pl.ds(rel_col * HALF, HALF)],
                )
            )
    xcols_copy = local(x_hbm.at[:, pl.ds(pl.multiple_of(z_hi * HALF, HALF), HALF)], xcols)

    barrier = pltpu.get_barrier_semaphore()
    greeted = [
        (0, 1, 0, 0),
        (0, -1, 0, 0),
        (0, 0, 0, 1),
        (1, 0, 0, 0),
        (-1, 0, 0, 0),
        (2, 0, 0, 0),
        (0, 0, 1, 0),
        (0, 0, -1, 0),
        (0, 0, 2, 0),
    ]
    for offset in greeted:
        pl.semaphore_signal(barrier, inc=1, device_id=device(*offset), device_id_type=MESH)
    pl.semaphore_wait(barrier, len(greeted))

    sent = []

    def send(src, dst, to):
        number = len(sent)
        copy = pltpu.make_async_remote_copy(
            src_ref=src,
            dst_ref=dst,
            send_sem=send_sem.at[number],
            recv_sem=recv_sem.at[number],
            device_id=to,
            device_id_type=MESH,
        )
        copy.start()
        sent.append(copy)
        return copy

    up, down, other = device(0, 1, 0, 0), device(0, -1, 0, 0), device(0, 0, 0, 1)
    low, high = pl.ds(0, ROWS // 2), pl.ds(ROWS // 2, ROWS // 2)

    def own_part(part):
        return x_hbm.at[pl.ds(pl.multiple_of(z_hi * ROWS + part * (ROWS // 2), ROWS // 2), ROWS // 2)]

    up_low = send(own_part(0), xg.at[0, 1, low], up)
    down_high = send(own_part(1), xg.at[0, 2, high], down)
    up_high = send(own_part(1), xg.at[0, 1, high], up)
    down_low = send(own_part(0), xg.at[0, 2, low], down)
    to_other = [send(own_rows, xg.at[1, 0], other)]
    up_low.wait_recv()
    far_low = send(xg.at[0, 1, low], xg.at[0, 3, low], up)
    down_high.wait_recv()
    far_high = send(xg.at[0, 2, high], xg.at[0, 3, high], down)
    up_high.wait_recv()
    to_other.append(send(xg.at[0, 1], xg.at[1, 1], other))
    down_low.wait_recv()
    to_other.append(send(xg.at[0, 2], xg.at[1, 2], other))
    own_copy.wait()
    for copy in w_copies:
        copy.wait()
    far_low.wait_recv()
    far_high.wait_recv()
    to_other.append(send(xg.at[0, 3], xg.at[1, 3], other))
    for copy in to_other:
        copy.wait_recv()

    def normed(value, gain):
        mean_square = jnp.mean(value * value, axis=1, keepdims=True)
        return value * lax.rsqrt(mean_square + EPS) * gain

    def keep(which, head, value):
        if which == 0:
            query = normed(value, qgain_ref[...])
            qtext[head] = query.astype(BF16)
            qbuf[head, 0] = (query * SCORE).astype(BF16)
        elif which == 1:
            kbuf[head, 0] = normed(value, kgain_ref[...]).astype(BF16)
        else:
            vbuf[head, 0] = value.T.astype(BF16)

    latents = xg[...].reshape(GROUP, WIDTH)
    near = {}

    def send_near(head):
        near[head] = [
            send(kbuf.at[head, 0], kbuf.at[head, 1], key_device(1)),
            send(vbuf.at[head, 0], vbuf.at[head, 1], key_device(1)),
            send(qbuf.at[head, 0], qbuf.at[head, 1], query_device(1)),
            send(kbuf.at[head, 0], kbuf.at[head, 2], key_device(-1)),
            send(vbuf.at[head, 0], vbuf.at[head, 2], key_device(-1)),
            send(qbuf.at[head, 0], qbuf.at[head, 2], query_device(-1)),
        ]

    done = 0
    for start in range(0, len(order), 2):
        pair = order[start : start + 2]
        product = jnp.dot(
            latents,
            wq[:, start * HD : (start + len(pair)) * HD],
            preferred_element_type=F32,
        )
        for i, (which, head) in enumerate(pair):
            keep(which, head, product[:, i * HD : (i + 1) * HD])
        while done < HEADS and start + len(pair) >= 3 * (done + 1):
            send_near(done)
            done += 1

    far = {}

    def send_far(head):
        for copy in near[head]:
            copy.wait_recv()
        a, b = pl.ds(0, GROUP // 2), pl.ds(GROUP // 2, GROUP // 2)
        va, vb = pl.ds(0, HD // 2), pl.ds(HD // 2, HD // 2)
        far[head] = [
            send(kbuf.at[head, 1, a], kbuf.at[head, 3, a], key_device(1)),
            send(vbuf.at[head, 1, va], vbuf.at[head, 3, va], key_device(1)),
            send(qbuf.at[head, 1, a], qbuf.at[head, 3, a], query_device(1)),
            send(kbuf.at[head, 2, b], kbuf.at[head, 3, b], key_device(-1)),
            send(vbuf.at[head, 2, vb], vbuf.at[head, 3, vb], key_device(-1)),
            send(qbuf.at[head, 2, b], qbuf.at[head, 3, b], query_device(-1)),
        ]

    text_copy.wait()

    def text_attention(head):
        columns = slice(head * HD, (head + 1) * HD)
        for half in range(2):
            scores = (
                lax.dot_general(text[half, 0, :, columns], qtext[head], NT, preferred_element_type=F32)
                * SCORE
            )
            valid = lax.broadcasted_iota(jnp.int32, scores.shape, 0) < lengths_ref[half]
            scores = jnp.where(valid, scores, -jnp.inf)
            top = jnp.max(scores, axis=0, keepdims=True)
            weights = jnp.exp2(scores - top)
            total = jnp.sum(weights, axis=0, keepdims=True)
            textout[head, half] = lax.dot_general(
                text[half, 1, :, columns], weights.astype(BF16), TN, preferred_element_type=F32
            )
            textstat[head, half, 0:1] = top
            textstat[head, half, 1:2] = total

    back = {}

    def attend(head):
        for copy in far[head]:
            copy.wait_recv()
        queries = qbuf[head].reshape(4 * GROUP, HD)
        top = total = weighted = None
        for slot in range(4):
            for at in range(0, GROUP, KEY_CHUNK):
                scores = lax.dot_general(
                    kbuf[head, slot, at : at + KEY_CHUNK], queries, NT, preferred_element_type=F32
                )
                chunk_top = jnp.max(scores, axis=0, keepdims=True)
                new_top = chunk_top if top is None else jnp.maximum(top, chunk_top)
                weights = jnp.exp2(scores - new_top)
                chunk_total = jnp.sum(weights, axis=0, keepdims=True)
                product = jnp.dot(
                    vbuf[head, slot, :, at : at + KEY_CHUNK],
                    weights.astype(BF16),
                    preferred_element_type=F32,
                )
                if top is None:
                    total, weighted = chunk_total, product
                else:
                    shrink = jnp.exp2(top - new_top)
                    total = total * shrink + chunk_total
                    weighted = weighted * shrink + product
                top = new_top
        result = weighted / total
        log_total = top + jnp.log2(total)
        for slot in range(4):
            part = result[:, slot * GROUP : (slot + 1) * GROUP]
            stat = log_total[:, slot * GROUP : (slot + 1) * GROUP]
            if slot == 0:
                oown[head] = part
                lown[head] = stat
            else:
                osend[head, slot - 1] = part.astype(BF16)
                lsend[head, slot - 1] = jnp.broadcast_to(stat, (8, GROUP))
        back[head] = []
        for slot, d, lands in ((3, 2, 3), (1, -1, 2), (2, 1, 1)):
            back[head].append(send(osend.at[head, slot - 1], orecv.at[head, lands - 1], query_device(d)))
            back[head].append(send(lsend.at[head, slot - 1], lrecv.at[head, lands - 1], query_device(d)))

    guidance = guidance_ref[0]
    swapped = []

    def combine(head):
        for copy in back[head]:
            copy.wait_recv()
        stats = [lown[head]] + [lrecv[head, i, 0:1] for i in range(3)]
        parts = [oown[head]] + [orecv[head, i].astype(F32) for i in range(3)]
        top = functools.reduce(jnp.maximum, stats)
        shares = [jnp.exp2(s - top) for s in stats]
        total = functools.reduce(jnp.add, shares)
        video = functools.reduce(jnp.add, [p * s for p, s in zip(parts, shares)]) / total
        video_log = top + jnp.log2(total)
        halves = []
        for half in range(2):
            text_top = textstat[head, half, 0:1]
            text_total = textstat[head, half, 1:2]
            both = jnp.maximum(video_log, text_top)
            a, b = jnp.exp2(video_log - both), jnp.exp2(text_top - both)
            scale = 1.0 / (a + b * text_total)
            halves.append(video * (a * scale) + textout[head, half] * (b * scale))
        guided = halves[1] + guidance * (halves[0] - halves[1])
        rows = guided.T.astype(BF16)
        abuf[:, head * HD : (head + 1) * HD] = rows[: GROUP // 2]
        asend[head] = rows[GROUP // 2 :]
        swapped.append(
            send(asend.at[head], abuf.at[:, pl.ds(OWN + head * HD, HD)], other)
        )

    send_far(0)
    for head in range(HEADS):
        text_attention(head)
    send_far(1)
    attend(0)
    send_far(2)
    attend(1)
    combine(0)
    attend(2)
    combine(1)
    combine(2)

    for copy in wo_copies:
        copy.wait()
    for copy in swapped:
        copy.wait_recv()
    attention = abuf[...]
    chunks = WIDTH // OUT_CHUNK
    far_sum, near_sum = [], []
    half_rows = ROWS // 2
    for j in range(chunks):
        columns = slice(j * OUT_CHUNK, (j + 1) * OUT_CHUNK)
        product = jnp.dot(attention, wo[:, columns], preferred_element_type=F32)
        pown[j] = product[:ROWS]
        dsend[j] = product[3 * ROWS :].astype(BF16)
        nsend[j, 0] = product[ROWS : 2 * ROWS].astype(BF16)
        nsend[j, 1] = product[2 * ROWS : 3 * ROWS].astype(BF16)
        far_sum.append(
            (
                send(dsend.at[j, low], drecv.at[j, 0], up),
                send(dsend.at[j, high], drecv.at[j, 1], down),
            )
        )
        near_sum.append(send(nsend.at[j, 1, high], nrecv.at[j, 0, high], up))
        near_sum.append(send(nsend.at[j, 0, low], nrecv.at[j, 1, low], down))
    for j in range(chunks):
        for copy in far_sum[j]:
            copy.wait_recv()
        nsend[j, 1, :half_rows] = (
            nsend[j, 1, :half_rows].astype(F32) + drecv[j, 0].astype(F32)
        ).astype(BF16)
        nsend[j, 0, half_rows:] = (
            nsend[j, 0, half_rows:].astype(F32) + drecv[j, 1].astype(F32)
        ).astype(BF16)
        near_sum.append(send(nsend.at[j, 1, low], nrecv.at[j, 0, low], up))
        near_sum.append(send(nsend.at[j, 0, high], nrecv.at[j, 1, high], down))

    xcols_copy.wait()
    position = index_ref[0]
    sigma_step = sigmas_ref[position + 1] - sigmas_ref[position]
    mine = pl.ds(pl.multiple_of(z_hi * ROWS, ROWS), ROWS)
    theirs = pl.ds(pl.multiple_of((1 - z_hi) * ROWS, ROWS), ROWS)
    exchanged = []
    for j in range(chunks):
        for k in (2 * j, 2 * j + 1, 2 * chunks + 2 * j, 2 * chunks + 2 * j + 1):
            near_sum[k].wait_recv()
        guided = pown[j] + nrecv[j, 0].astype(F32) + nrecv[j, 1].astype(F32)
        if j < chunks // 2:
            csend[j] = guided.astype(BF16)
            exchanged.append(send(csend.at[j], crecv.at[j], device(0, 0, 2, 0)))
        else:
            at = (j - chunks // 2) * OUT_CHUNK
            columns = pl.ds(at, OUT_CHUNK)
            guided_ref[mine, columns] = guided.astype(BF16)
            next_ref[mine, columns] = (
                xcols[mine, columns].astype(F32) + sigma_step * guided
            ).astype(BF16)
    for j in range(chunks // 2):
        exchanged[j].wait_recv()
        columns = pl.ds(j * OUT_CHUNK, OUT_CHUNK)
        guided = crecv[j]
        guided_ref[theirs, columns] = guided
        next_ref[theirs, columns] = (
            xcols[theirs, columns].astype(F32) + sigma_step * guided.astype(F32)
        ).astype(BF16)
    for copy in sent:
        copy.wait_send()


def per_device(latents, w_qkv, w_out, q_gain, k_gain, text_kv, text_lengths, sigmas, step_index, guidance):
    any_space = pl.BlockSpec(memory_space=pl.ANY)
    vmem = pl.BlockSpec(memory_space=pltpu.VMEM)
    smem = pl.BlockSpec(memory_space=pltpu.SMEM)
    chunks = WIDTH // OUT_CHUNK
    out = jax.ShapeDtypeStruct((2 * ROWS, HALF), BF16)
    return pl.pallas_call(
        step_kernel,
        name="denoising_step",
        out_shape=(out, out),
        in_specs=[any_space] * 4 + [vmem] * 2 + [smem] * 4,
        out_specs=(vmem, vmem),
        scratch_shapes=[
            pltpu.VMEM((2, 4, ROWS, WIDTH), BF16),
            pltpu.VMEM((WIDTH, 3 * OWN), BF16),
            pltpu.VMEM((2 * OWN, WIDTH), BF16),
            pltpu.VMEM((2, 2, 256, OWN), BF16),
            pltpu.VMEM((2 * ROWS, HALF), BF16),
            pltpu.VMEM((HEADS, 4, GROUP, HD), BF16),
            pltpu.VMEM((HEADS, 4, GROUP, HD), BF16),
            pltpu.VMEM((HEADS, 4, HD, GROUP), BF16),
            pltpu.VMEM((HEADS, GROUP, HD), BF16),
            pltpu.VMEM((HEADS, 2, HD, GROUP), F32),
            pltpu.VMEM((HEADS, 2, 8, GROUP), F32),
            pltpu.VMEM((HEADS, 3, HD, GROUP), BF16),
            pltpu.VMEM((HEADS, 3, HD, GROUP), BF16),
            pltpu.VMEM((HEADS, 3, 8, GROUP), F32),
            pltpu.VMEM((HEADS, 3, 8, GROUP), F32),
            pltpu.VMEM((HEADS, HD, GROUP), F32),
            pltpu.VMEM((HEADS, 1, GROUP), F32),
            pltpu.VMEM((HEADS, GROUP // 2, HD), BF16),
            pltpu.VMEM((GROUP // 2, 2 * OWN), BF16),
            pltpu.VMEM((chunks, ROWS, OUT_CHUNK), BF16),
            pltpu.VMEM((chunks, 2, ROWS // 2, OUT_CHUNK), BF16),
            pltpu.VMEM((chunks, 2, ROWS, OUT_CHUNK), BF16),
            pltpu.VMEM((chunks, 2, ROWS, OUT_CHUNK), BF16),
            pltpu.VMEM((chunks, ROWS, OUT_CHUNK), F32),
            pltpu.VMEM((chunks // 2, ROWS, OUT_CHUNK), BF16),
            pltpu.VMEM((chunks // 2, ROWS, OUT_CHUNK), BF16),
            pltpu.SemaphoreType.DMA((16,)),
            pltpu.SemaphoreType.DMA((MESSAGES,)),
            pltpu.SemaphoreType.DMA((MESSAGES,)),
        ],
        compiler_params=pltpu.CompilerParams(
            collective_id=0, has_side_effects=True, vmem_limit_bytes=60 * 2**20
        ),
        cost_estimate=pl.CostEstimate(
            flops=12 * 10**9, bytes_accessed=15 * 10**6, transcendentals=14 * 10**6
        ),
    )(
        latents,
        jnp.transpose(w_qkv, (1, 0, 2)),
        w_out,
        text_kv,
        q_gain.reshape(1, HD),
        k_gain.reshape(1, HD),
        text_lengths,
        sigmas,
        step_index,
        guidance,
    )


def solution(mesh):
    placed = (
        P(("blk", "ulysses"), None),
        P(None, None, "ulysses"),
        P("ulysses", None),
        P(),
        P(),
        P(None, None, None, "ulysses"),
        P(),
        P(),
        P(),
        P(),
    )
    return jax.shard_map(
        per_device,
        mesh=mesh,
        in_specs=placed,
        out_specs=(P(("blk", "ulysses"), "cfg"), P(("blk", "ulysses"), "cfg")),
        check_vma=False,
    )
```

```python
import functools
import math

import jax
import jax.numpy as jnp
from jax import lax
from jax.experimental import pallas as pl
from jax.experimental.pallas import tpu as pltpu
from jax.sharding import PartitionSpec as P

HD = 128
EPS = 1e-06
LOG2E = math.log2(math.e)
SCORE = LOG2E / math.sqrt(HD)
MESH = pl.DeviceIdType.MESH
NT = (((1,), (1,)), ((), ()))
TN = (((0,), (0,)), ((), ()))
F32 = jnp.float32
BF16 = jnp.bfloat16

HEADS = 3
ROWS = 64
PART = ROWS // 2
UNITS = 4
UNIT = 2 * ROWS
QUERIES = 4 * UNIT
WIDTH = 3072
HALF = WIDTH // 2
OWN = HEADS * HD
MESSAGES = 96


def place():
    blk = lax.axis_index("blk")
    z_hi = lax.axis_index("cfg")
    core = lax.rem(blk, 2)
    x = lax.rem(lax.div(blk, 2), 4)
    z = z_hi * 2 + lax.div(blk, 8)
    return x, lax.axis_index("ulysses"), z, core, z_hi


def step_kernel(
    x_hbm,
    wqkv_hbm,
    wout_hbm,
    text_hbm,
    qgain_ref,
    kgain_ref,
    lengths_ref,
    sigmas_ref,
    index_ref,
    guidance_ref,
    guided_ref,
    next_ref,
    xg,
    wq,
    wo,
    text,
    xcols,
    qs,
    kv,
    qtext,
    textout,
    textstat,
    osend,
    orecv,
    lsend,
    lrecv,
    oown,
    lown,
    asend,
    abuf,
    dsend,
    drecv,
    nsend,
    nrecv,
    local_sem,
    send_sem,
    recv_sem,
):
    x, y, z, core, z_hi = place()

    def device(dx, dy, dz, dc):
        tx = lax.rem(x + dx + 4, 4)
        ty = lax.rem(y + dy + 4, 4)
        tz = lax.rem(z + dz + 4, 4)
        tc = lax.rem(core + dc, 2)
        return (lax.div(tz, 2), lax.rem(tz, 2) * 8 + tx * 2 + tc, ty)

    def key_device(d):
        return device((1 - core) * d, 0, core * d, 0)

    def query_device(d):
        return device(core * d, 0, (1 - core) * d, 0)

    locals_started = []

    def local(src, dst):
        copy = pltpu.make_async_copy(src, dst, local_sem.at[len(locals_started)])
        copy.start()
        locals_started.append(copy)
        return copy

    own_rows = x_hbm.at[pl.ds(pl.multiple_of(z_hi * ROWS, ROWS), ROWS)]
    own_copy = local(own_rows, xg.at[0, 0])
    own_col = pl.multiple_of(core * OWN, OWN)
    w_copies = [
        local(wqkv_hbm.at[which, :, pl.ds(own_col, OWN)], wq.at[:, pl.ds(at * OWN, OWN)])
        for at, which in enumerate((1, 2, 0))
    ]
    text_copy = local(text_hbm.at[:, :, :, pl.ds(own_col, OWN)], text)
    columns_here = pl.ds(pl.multiple_of(z_hi * HALF, HALF), HALF)
    wo_copies = [
        local(wout_hbm.at[pl.ds(pl.multiple_of(c * OWN, OWN), OWN), columns_here], wo.at[pl.ds(at * OWN, OWN)])
        for at, c in enumerate((core, 1 - core))
    ]
    xcols_copy = local(x_hbm.at[:, columns_here], xcols)

    barrier = pltpu.get_barrier_semaphore()
    greeted = [
        (0, 1, 0, 0),
        (0, -1, 0, 0),
        (0, 0, 0, 1),
        (1, 0, 0, 0),
        (-1, 0, 0, 0),
        (2, 0, 0, 0),
        (0, 0, 1, 0),
        (0, 0, -1, 0),
        (0, 0, 2, 0),
        (0, 0, 2, 1),
    ]
    for offset in greeted:
        pl.semaphore_signal(barrier, inc=1, device_id=device(*offset), device_id_type=MESH)
    pl.semaphore_wait(barrier, len(greeted))

    sent = []

    def send(src, dst, to):
        number = len(sent)
        copy = pltpu.make_async_remote_copy(
            src_ref=src,
            dst_ref=dst,
            send_sem=send_sem.at[number],
            recv_sem=recv_sem.at[number],
            device_id=to,
            device_id_type=MESH,
        )
        copy.start()
        sent.append(copy)
        return copy

    up, down, other = device(0, 1, 0, 0), device(0, -1, 0, 0), device(0, 0, 0, 1)
    low, high = pl.ds(0, PART), pl.ds(PART, PART)

    def own_part(part):
        return x_hbm.at[pl.ds(pl.multiple_of(z_hi * ROWS + part * PART, PART), PART)]

    up_first = send(own_part(0), xg.at[1, 0, low], up)
    down_first = send(own_part(1), xg.at[1, 0, high], down)
    across = [send(own_rows, xg.at[0, 1], other)]
    up_second = send(own_part(1), xg.at[2, 0, low], up)
    down_second = send(own_part(0), xg.at[2, 0, high], down)

    def normed(value, gain):
        mean_square = jnp.mean(value * value, axis=1, keepdims=True)
        return value * lax.rsqrt(mean_square + EPS) * gain

    def project(unit):
        product = jnp.dot(
            xg[unit].reshape(UNIT, WIDTH), wq[...], preferred_element_type=F32
        )
        for head in range(HEADS):
            at = head * HD
            key = normed(product[:, at : at + HD], kgain_ref[...])
            kv[0, unit, 0, head] = key.astype(BF16)
            kv[0, unit, 1, head] = product[:, OWN + at : OWN + at + HD].T.astype(BF16)
            query = normed(product[:, 2 * OWN + at : 2 * OWN + at + HD], qgain_ref[...])
            qtext[unit, head] = query.astype(BF16)
            qs[0, unit, head] = (query * SCORE).astype(BF16)

    near_kv, near_q, far_kv, far_q = {}, {}, {}, {}

    def send_near_kv(unit):
        near_kv[unit] = [
            send(kv.at[0, unit], kv.at[1, unit], key_device(1)),
            send(kv.at[0, unit], kv.at[2, unit], key_device(-1)),
        ]

    def send_near_q(unit):
        near_q[unit] = [
            send(qs.at[0, unit], qs.at[1, unit], query_device(1)),
            send(qs.at[0, unit], qs.at[2, unit], query_device(-1)),
        ]

    def send_far_kv(unit):
        for copy in near_kv[unit]:
            copy.wait_recv()
        far_kv[unit] = [
            send(kv.at[1, unit, 0], kv.at[3, unit, 0], key_device(1)),
            send(kv.at[2, unit, 1], kv.at[3, unit, 1], key_device(-1)),
        ]

    def send_far_q(unit):
        for copy in near_q[unit]:
            copy.wait_recv()
        first, second = pl.ds(0, UNIT // 2), pl.ds(UNIT // 2, UNIT // 2)
        far_q[unit] = [
            send(qs.at[1, unit, :, first], qs.at[3, unit, :, first], query_device(1)),
            send(qs.at[2, unit, :, second], qs.at[3, unit, :, second], query_device(-1)),
        ]

    lsend[...] = jnp.zeros_like(lsend)
    for copy in w_copies:
        copy.wait()
    own_copy.wait()
    across[0].wait_recv()
    project(0)
    send_near_kv(0)
    send_near_q(0)
    up_first.wait_recv()
    far_up = send(xg.at[1, 0, low], xg.at[3, 0, low], up)
    down_first.wait_recv()
    far_down = send(xg.at[1, 0, high], xg.at[3, 0, high], down)
    across.append(send(xg.at[1, 0], xg.at[1, 1], other))
    send_far_kv(0)
    send_far_q(0)
    across[1].wait_recv()
    project(1)
    send_near_kv(1)
    send_near_q(1)
    up_second.wait_recv()
    down_second.wait_recv()
    across.append(send(xg.at[2, 0], xg.at[2, 1], other))
    across[2].wait_recv()
    project(2)
    send_near_kv(2)
    far_up.wait_recv()
    far_down.wait_recv()
    across.append(send(xg.at[3, 0], xg.at[3, 1], other))
    send_far_kv(1)
    across[3].wait_recv()
    project(3)
    send_near_kv(3)
    send_near_q(3)
    send_far_q(1)
    send_far_kv(2)

    def text_attention(head):
        columns = slice(head * HD, (head + 1) * HD)
        queries = qtext[:, head].reshape(UNITS * UNIT, HD)
        for half in range(2):
            scores = (
                lax.dot_general(text[half, 0, :, columns], queries, NT, preferred_element_type=F32)
                * SCORE
            )
            valid = lax.broadcasted_iota(jnp.int32, scores.shape, 0) < lengths_ref[half]
            scores = jnp.where(valid, scores, -jnp.inf)
            top = jnp.max(scores, axis=0, keepdims=True)
            weights = jnp.exp2(scores - top)
            total = jnp.sum(weights, axis=0, keepdims=True)
            textout[head, half] = lax.dot_general(
                text[half, 1, :, columns], weights.astype(BF16), TN, preferred_element_type=F32
            )
            textstat[head, half, 0:1] = top
            textstat[head, half, 1:2] = total

    back = {unit: [] for unit in range(UNITS)}

    def attend(unit, heads=range(HEADS)):
        steps = [(head, pair) for head in heads for pair in range(2)]
        scores_of = {}

        def score(head, pair):
            keys = kv[2 * pair : 2 * pair + 2, :, 0, head].reshape(2 * UNITS * UNIT, HD)
            queries = qs[:, unit, head].reshape(QUERIES, HD)
            return lax.dot_general(keys, queries, NT, preferred_element_type=F32)

        scores_of[steps[0]] = score(*steps[0])
        for i, (head, pair) in enumerate(steps):
            if i + 1 < len(steps):
                scores_of[steps[i + 1]] = score(*steps[i + 1])
            scores = scores_of.pop((head, pair))
            new_top = jnp.max(scores, axis=0, keepdims=True)
            if pair:
                new_top = jnp.maximum(new_top, top)
            weights = jnp.exp2(scores - new_top)
            part_total = jnp.sum(weights, axis=0, keepdims=True)
            values = jnp.concatenate(
                [kv[slot, u, 1, head] for slot in (2 * pair, 2 * pair + 1) for u in range(UNITS)], axis=1
            )
            product = jnp.dot(values, weights.astype(BF16), preferred_element_type=F32)
            if pair:
                shrink = jnp.exp2(top - new_top)
                part_total = total * shrink + part_total
                product = weighted * shrink + product
            top, total, weighted = new_top, part_total, product
            if pair:
                result = weighted / total
                log_total = top + jnp.log2(total)
                for slot in range(4):
                    part = result[:, slot * UNIT : (slot + 1) * UNIT]
                    stat = log_total[:, slot * UNIT : (slot + 1) * UNIT]
                    if slot == 0:
                        oown[unit, head] = part
                        lown[unit, head : head + 1] = stat
                    else:
                        osend[unit, slot - 1, head] = part.astype(BF16)
                        lsend[unit, slot - 1, head : head + 1] = stat

    def send_back(unit):
        for slot, d, lands in ((3, 2, 3), (1, -1, 2), (2, 1, 1)):
            back[unit].append(send(osend.at[unit, slot - 1], orecv.at[unit, lands - 1], query_device(d)))
            back[unit].append(send(lsend.at[unit, slot - 1], lrecv.at[unit, lands - 1], query_device(d)))

    guidance = guidance_ref[0]
    swapped = {}

    def combine(unit):
        for copy in back[unit]:
            copy.wait_recv()
        span = slice(unit * UNIT, (unit + 1) * UNIT)
        for head in range(HEADS):
            stats = [lown[unit, head : head + 1]] + [lrecv[unit, i, head : head + 1] for i in range(3)]
            parts = [oown[unit, head]] + [orecv[unit, i, head].astype(F32) for i in range(3)]
            top = functools.reduce(jnp.maximum, stats)
            shares = [jnp.exp2(s - top) for s in stats]
            total = functools.reduce(jnp.add, shares)
            video = functools.reduce(jnp.add, [p * s for p, s in zip(parts, shares)]) / total
            video_log = top + jnp.log2(total)
            halves = []
            for half in range(2):
                text_top = textstat[head, half, 0:1, span]
                text_total = textstat[head, half, 1:2, span]
                both = jnp.maximum(video_log, text_top)
                a, b = jnp.exp2(video_log - both), jnp.exp2(text_top - both)
                scale = 1.0 / (a + b * text_total)
                halves.append(video * (a * scale) + textout[head, half, :, span] * (b * scale))
            guided = halves[1] + guidance * (halves[0] - halves[1])
            rows = guided.T.astype(BF16)
            columns = slice(head * HD, (head + 1) * HD)
            asend[unit, 0, :, columns] = rows[:ROWS]
            asend[unit, 1, :, columns] = rows[ROWS:]
        abuf[unit, 0, :, :OWN] = asend[unit, 0]
        first, second = pl.ds(0, OWN), pl.ds(OWN, OWN)
        swapped[unit] = [
            send(asend.at[unit, 0], abuf.at[unit, 1, :, first], device(0, 0, 2, 0)),
            send(asend.at[unit, 1], abuf.at[unit, 1, :, second], device(0, 0, 2, 1)),
            send(asend.at[unit, 1], abuf.at[unit, 0, :, second], other),
        ]

    def output(unit):
        for copy in swapped[unit]:
            copy.wait_recv()
        return jnp.dot(
            abuf[unit].reshape(UNIT, 2 * OWN), wo[...], preferred_element_type=F32
        ).reshape(2, ROWS, HALF)

    text_copy.wait()
    for head in range(HEADS):
        text_attention(head)
    send_far_kv(3)
    send_far_q(3)
    send_near_q(2)
    for unit in range(UNITS):
        for copy in far_kv[unit]:
            copy.wait_recv()
    for copy in far_q[3]:
        copy.wait_recv()
    attend(3)
    send_back(3)
    send_far_q(2)
    for copy in far_q[1]:
        copy.wait_recv()
    attend(1)
    send_back(1)
    combine(3)
    for copy in far_q[2]:
        copy.wait_recv()
    attend(2)
    send_back(2)
    for copy in wo_copies:
        copy.wait()
    dsend[...] = output(3).astype(BF16)
    far_sum = [
        send(dsend.at[:, low], drecv.at[0], up),
        send(dsend.at[:, high], drecv.at[1], down),
    ]
    combine(1)
    for copy in far_q[0]:
        copy.wait_recv()
    attend(0, (0, 1))
    nsend[0] = output(1).astype(BF16)
    near_sum = [
        send(nsend.at[0, :, low], nrecv.at[0, :, low], down),
        send(nsend.at[0, :, high], nrecv.at[1, :, high], up),
    ]
    combine(2)
    attend(0, (2,))
    send_back(0)
    product = output(2)
    for copy in far_sum:
        copy.wait_recv()
    nsend[1, :, :PART] = (product[:, :PART] + drecv[1].astype(F32)).astype(BF16)
    nsend[1, :, PART:] = (product[:, PART:] + drecv[0].astype(F32)).astype(BF16)
    near_sum += [
        send(nsend.at[1, :, low], nrecv.at[0, :, high], down),
        send(nsend.at[1, :, high], nrecv.at[1, :, low], up),
    ]
    combine(0)
    xcols_copy.wait()
    position = index_ref[0]
    sigma_step = sigmas_ref[position + 1] - sigmas_ref[position]
    product = output(0)
    for copy in near_sum:
        copy.wait_recv()
    guided = product + nrecv[0].astype(F32) + nrecv[1].astype(F32)
    for at, half in enumerate((z_hi, 1 - z_hi)):
        rows = pl.ds(pl.multiple_of(half * ROWS, ROWS), ROWS)
        guided_ref[rows] = guided[at].astype(BF16)
        next_ref[rows] = (xcols[rows].astype(F32) + sigma_step * guided[at]).astype(BF16)
    for copy in sent:
        copy.wait_send()


def per_device(latents, w_qkv, w_out, q_gain, k_gain, text_kv, text_lengths, sigmas, step_index, guidance):
    any_space = pl.BlockSpec(memory_space=pl.ANY)
    vmem = pl.BlockSpec(memory_space=pltpu.VMEM)
    smem = pl.BlockSpec(memory_space=pltpu.SMEM)
    out = jax.ShapeDtypeStruct((2 * ROWS, HALF), BF16)
    return pl.pallas_call(
        step_kernel,
        name="denoising_step",
        out_shape=(out, out),
        in_specs=[any_space] * 4 + [vmem] * 2 + [smem] * 4,
        out_specs=(vmem, vmem),
        scratch_shapes=[
            pltpu.VMEM((UNITS, 2, ROWS, WIDTH), BF16),
            pltpu.VMEM((WIDTH, 3 * OWN), BF16),
            pltpu.VMEM((2 * OWN, HALF), BF16),
            pltpu.VMEM((2, 2, 256, OWN), BF16),
            pltpu.VMEM((2 * ROWS, HALF), BF16),
            pltpu.VMEM((4, UNITS, HEADS, UNIT, HD), BF16),
            pltpu.VMEM((4, UNITS, 2, HEADS, UNIT, HD), BF16),
            pltpu.VMEM((UNITS, HEADS, UNIT, HD), BF16),
            pltpu.VMEM((HEADS, 2, HD, UNITS * UNIT), F32),
            pltpu.VMEM((HEADS, 2, 8, UNITS * UNIT), F32),
            pltpu.VMEM((UNITS, 3, HEADS, HD, UNIT), BF16),
            pltpu.VMEM((UNITS, 3, HEADS, HD, UNIT), BF16),
            pltpu.VMEM((UNITS, 3, 8, UNIT), F32),
            pltpu.VMEM((UNITS, 3, 8, UNIT), F32),
            pltpu.VMEM((UNITS, HEADS, HD, UNIT), F32),
            pltpu.VMEM((UNITS, 8, UNIT), F32),
            pltpu.VMEM((UNITS, 2, ROWS, OWN), BF16),
            pltpu.VMEM((UNITS, 2, ROWS, 2 * OWN), BF16),
            pltpu.VMEM((2, ROWS, HALF), BF16),
            pltpu.VMEM((2, 2, PART, HALF), BF16),
            pltpu.VMEM((2, 2, ROWS, HALF), BF16),
            pltpu.VMEM((2, 2, ROWS, HALF), BF16),
            pltpu.SemaphoreType.DMA((16,)),
            pltpu.SemaphoreType.DMA((MESSAGES,)),
            pltpu.SemaphoreType.DMA((MESSAGES,)),
        ],
        compiler_params=pltpu.CompilerParams(
            collective_id=0, has_side_effects=True, vmem_limit_bytes=60 * 2**20
        ),
        cost_estimate=pl.CostEstimate(
            flops=12 * 10**9, bytes_accessed=15 * 10**6, transcendentals=14 * 10**6
        ),
    )(
        latents,
        jnp.transpose(w_qkv, (1, 0, 2)),
        w_out,
        text_kv,
        q_gain.reshape(1, HD),
        k_gain.reshape(1, HD),
        text_lengths,
        sigmas,
        step_index,
        guidance,
    )


def solution(mesh):
    placed = (
        P(("blk", "ulysses"), None),
        P(None, None, "ulysses"),
        P("ulysses", None),
        P(),
        P(),
        P(None, None, None, "ulysses"),
        P(),
        P(),
        P(),
        P(),
    )
    return jax.shard_map(
        per_device,
        mesh=mesh,
        in_specs=placed,
        out_specs=(P(("blk", "ulysses"), "cfg"), P(("blk", "ulysses"), "cfg")),
        check_vma=False,
    )
```

```python
import functools
import math

import jax
import jax.numpy as jnp
from jax import lax
from jax.experimental import pallas as pl
from jax.experimental.pallas import tpu as pltpu
from jax.sharding import PartitionSpec as P

HD = 128
EPS = 1e-06
LOG2E = math.log2(math.e)
SCORE = LOG2E / math.sqrt(HD)
MESH = pl.DeviceIdType.MESH
NT = (((1,), (1,)), ((), ()))
TN = (((0,), (0,)), ((), ()))
F32 = jnp.float32
BF16 = jnp.bfloat16

HEADS = 3
ROWS = 64
PART = ROWS // 2
UNITS = 4
UNIT = 2 * ROWS
QUERIES = 4 * UNIT
WIDTH = 3072
HALF = WIDTH // 2
OWN = HEADS * HD
STAT = 16
SUM_COLUMNS = 768
MESSAGES = 128


def place():
    blk = lax.axis_index("blk")
    z_hi = lax.axis_index("cfg")
    core = lax.rem(blk, 2)
    x = lax.rem(lax.div(blk, 2), 4)
    z = z_hi * 2 + lax.div(blk, 8)
    return x, lax.axis_index("ulysses"), z, core, z_hi


def step_kernel(
    x_hbm,
    wqkv_hbm,
    wout_hbm,
    text_hbm,
    qgain_ref,
    kgain_ref,
    lengths_ref,
    sigmas_ref,
    index_ref,
    guidance_ref,
    guided_ref,
    next_ref,
    xg,
    wq,
    wo,
    text,
    xcols,
    qs,
    kv,
    qtext,
    textout,
    textstat,
    osend,
    orecv,
    oown,
    lown,
    asend,
    abuf,
    dsend,
    drecv,
    nsend,
    nrecv,
    local_sem,
    send_sem,
    recv_sem,
):
    x, y, z, core, z_hi = place()

    def device(dx, dy, dz, dc):
        tx = lax.rem(x + dx + 4, 4)
        ty = lax.rem(y + dy + 4, 4)
        tz = lax.rem(z + dz + 4, 4)
        tc = lax.rem(core + dc, 2)
        return (lax.div(tz, 2), lax.rem(tz, 2) * 8 + tx * 2 + tc, ty)

    def key_device(d):
        return device((1 - core) * d, 0, core * d, 0)

    def query_device(d):
        return device(core * d, 0, (1 - core) * d, 0)

    locals_started = []

    def local(src, dst):
        copy = pltpu.make_async_copy(src, dst, local_sem.at[len(locals_started)])
        copy.start()
        locals_started.append(copy)
        return copy

    own_rows = x_hbm.at[pl.ds(pl.multiple_of(z_hi * ROWS, ROWS), ROWS)]
    own_copy = local(own_rows, xg.at[0, 0])
    own_col = pl.multiple_of(core * OWN, OWN)
    w_copies = [
        local(wqkv_hbm.at[which, :, pl.ds(own_col, OWN)], wq.at[:, pl.ds(at * OWN, OWN)])
        for at, which in enumerate((1, 2, 0))
    ]
    text_copy = local(text_hbm.at[:, :, :, pl.ds(own_col, OWN)], text)
    columns_here = pl.ds(pl.multiple_of(z_hi * HALF, HALF), HALF)
    wo_copies = [
        local(wout_hbm.at[pl.ds(pl.multiple_of(c * OWN, OWN), OWN), columns_here], wo.at[pl.ds(at * OWN, OWN)])
        for at, c in enumerate((core, 1 - core))
    ]
    xcols_copy = local(x_hbm.at[:, columns_here], xcols)

    barrier = pltpu.get_barrier_semaphore()
    greeted = [
        (0, 1, 0, 0),
        (0, -1, 0, 0),
        (0, 0, 0, 1),
        (1, 0, 0, 0),
        (-1, 0, 0, 0),
        (2, 0, 0, 0),
        (0, 0, 1, 0),
        (0, 0, -1, 0),
        (0, 0, 2, 0),
        (0, 0, 2, 1),
    ]
    for offset in greeted:
        pl.semaphore_signal(barrier, inc=1, device_id=device(*offset), device_id_type=MESH)
    pl.semaphore_wait(barrier, len(greeted))

    sent = []

    def send(src, dst, to):
        number = len(sent)
        copy = pltpu.make_async_remote_copy(
            src_ref=src,
            dst_ref=dst,
            send_sem=send_sem.at[number],
            recv_sem=recv_sem.at[number],
            device_id=to,
            device_id_type=MESH,
        )
        copy.start()
        sent.append(copy)
        return copy

    up, down, other = device(0, 1, 0, 0), device(0, -1, 0, 0), device(0, 0, 0, 1)
    low, high = pl.ds(0, PART), pl.ds(PART, PART)

    def own_part(part):
        return x_hbm.at[pl.ds(pl.multiple_of(z_hi * ROWS + part * PART, PART), PART)]

    up_first = send(own_part(0), xg.at[1, 0, low], up)
    down_first = send(own_part(1), xg.at[1, 0, high], down)
    across = [send(own_rows, xg.at[0, 1], other)]
    up_second = send(own_part(1), xg.at[2, 0, low], up)
    down_second = send(own_part(0), xg.at[2, 0, high], down)

    def normed(value, gain):
        mean_square = jnp.mean(value * value, axis=1, keepdims=True)
        return value * lax.rsqrt(mean_square + EPS) * gain

    def project(unit):
        product = jnp.dot(
            xg[unit].reshape(UNIT, WIDTH), wq[...], preferred_element_type=F32
        )
        for head in range(HEADS):
            at = head * HD
            key = normed(product[:, at : at + HD], kgain_ref[...])
            kv[0, unit, 0, head] = key.astype(BF16)
            kv[0, unit, 1, head] = product[:, OWN + at : OWN + at + HD].T.astype(BF16)
            query = normed(product[:, 2 * OWN + at : 2 * OWN + at + HD], qgain_ref[...])
            qtext[unit, head] = query.astype(BF16)
            qs[0, unit, head] = (query * SCORE).astype(BF16)

    near_kv, near_q, far_kv, far_q = {}, {}, {}, {}

    def send_near_kv(unit):
        near_kv[unit] = [
            send(kv.at[0, unit], kv.at[1, unit], key_device(1)),
            send(kv.at[0, unit], kv.at[2, unit], key_device(-1)),
        ]

    def send_near_q(unit):
        near_q[unit] = [
            send(qs.at[0, unit], qs.at[1, unit], query_device(1)),
            send(qs.at[0, unit], qs.at[2, unit], query_device(-1)),
        ]

    def send_far_kv(unit):
        for copy in near_kv[unit]:
            copy.wait_recv()
        far_kv[unit] = [
            send(kv.at[1, unit, 0], kv.at[3, unit, 0], key_device(1)),
            send(kv.at[2, unit, 1], kv.at[3, unit, 1], key_device(-1)),
        ]

    def send_far_q(unit):
        for copy in near_q[unit]:
            copy.wait_recv()
        first, second = pl.ds(0, UNIT // 2), pl.ds(UNIT // 2, UNIT // 2)
        far_q[unit] = [
            send(qs.at[1, unit, :, first], qs.at[3, unit, :, first], query_device(1)),
            send(qs.at[2, unit, :, second], qs.at[3, unit, :, second], query_device(-1)),
        ]

    for copy in w_copies:
        copy.wait()
    own_copy.wait()
    across[0].wait_recv()
    project(0)
    send_near_kv(0)
    send_near_q(0)
    up_first.wait_recv()
    far_up = send(xg.at[1, 0, low], xg.at[3, 0, low], up)
    down_first.wait_recv()
    far_down = send(xg.at[1, 0, high], xg.at[3, 0, high], down)
    across.append(send(xg.at[1, 0], xg.at[1, 1], other))
    across[1].wait_recv()
    project(1)
    send_near_kv(1)
    send_near_q(1)
    send_far_kv(0)
    send_far_q(0)
    up_second.wait_recv()
    down_second.wait_recv()
    across.append(send(xg.at[2, 0], xg.at[2, 1], other))
    across[2].wait_recv()
    project(2)
    send_near_kv(2)
    send_far_kv(1)
    send_far_q(1)
    far_up.wait_recv()
    far_down.wait_recv()
    across.append(send(xg.at[3, 0], xg.at[3, 1], other))
    across[3].wait_recv()
    project(3)
    send_near_kv(3)
    send_near_q(3)
    send_far_kv(2)

    def text_attention(head):
        columns = slice(head * HD, (head + 1) * HD)
        queries = qtext[:, head].reshape(UNITS * UNIT, HD)
        for half in range(2):
            scores = (
                lax.dot_general(text[half, 0, :, columns], queries, NT, preferred_element_type=F32)
                * SCORE
            )
            valid = lax.broadcasted_iota(jnp.int32, scores.shape, 0) < lengths_ref[half]
            scores = jnp.where(valid, scores, -jnp.inf)
            top = jnp.max(scores, axis=0, keepdims=True)
            weights = jnp.exp2(scores - top)
            total = jnp.sum(weights, axis=0, keepdims=True)
            textout[head, half] = lax.dot_general(
                text[half, 1, :, columns], weights.astype(BF16), TN, preferred_element_type=F32
            )
            textstat[head, half, 0:1] = top
            textstat[head, half, 1:2] = total

    back = {}

    def attend(unit, heads, sends):
        steps = [(head, pair) for head in heads for pair in range(2)]
        scores_of = {}

        def score(head, pair):
            keys = kv[2 * pair : 2 * pair + 2, :, 0, head].reshape(2 * UNITS * UNIT, HD)
            queries = qs[:, unit, head].reshape(QUERIES, HD)
            return lax.dot_general(keys, queries, NT, preferred_element_type=F32)

        scores_of[steps[0]] = score(*steps[0])
        for n, (head, pair) in enumerate(steps):
            if n + 1 < len(steps):
                scores_of[steps[n + 1]] = score(*steps[n + 1])
            scores = scores_of.pop((head, pair))
            new_top = jnp.max(scores, axis=0, keepdims=True)
            if pair:
                new_top = jnp.maximum(new_top, top)
            weights = jnp.exp2(scores - new_top)
            part_total = jnp.sum(weights, axis=0, keepdims=True)
            values = jnp.concatenate(
                [kv[slot, u, 1, head] for slot in (2 * pair, 2 * pair + 1) for u in range(UNITS)], axis=1
            )
            product = jnp.dot(values, weights.astype(BF16), preferred_element_type=F32)
            if pair:
                shrink = jnp.exp2(top - new_top)
                part_total = total * shrink + part_total
                product = weighted * shrink + product
            top, total, weighted = new_top, part_total, product
            if not pair:
                continue
            result = weighted / total
            log_total = top + jnp.log2(total)
            row = lax.broadcasted_iota(jnp.int32, (STAT, UNIT), 0)
            for slot in range(4):
                part = result[:, slot * UNIT : (slot + 1) * UNIT]
                stat = log_total[:, slot * UNIT : (slot + 1) * UNIT]
                if slot == 0:
                    oown[unit, head] = part
                    lown[unit, head : head + 1] = stat
                else:
                    first = stat.astype(BF16).astype(F32)
                    second = (stat - first).astype(BF16).astype(F32)
                    third = stat - first - second
                    osend[unit, slot - 1, head, :HD] = part.astype(BF16)
                    osend[unit, slot - 1, head, HD:] = jnp.where(
                        row == 0, first, jnp.where(row == 1, second, third)
                    ).astype(BF16)
            for group in sends:
                if head == group[-1]:
                    send_back(unit, group)

    def send_back(unit, group):
        span = pl.ds(group[0], len(group))
        back[unit, group] = [
            send(osend.at[unit, slot - 1, span], orecv.at[unit, lands - 1, span], query_device(d))
            for slot, d, lands in ((3, 2, 3), (1, -1, 2), (2, 1, 1))
        ]

    guidance = guidance_ref[0]
    swapped = {unit: [] for unit in range(UNITS)}

    def combine(unit, group):
        for copy in back[unit, group]:
            copy.wait_recv()
        span = slice(unit * UNIT, (unit + 1) * UNIT)
        for head in group:
            stats = [lown[unit, head : head + 1]]
            parts = [oown[unit, head]]
            for i in range(3):
                log_parts = orecv[unit, i, head, HD:].astype(F32)
                stats.append(log_parts[0:1] + log_parts[1:2] + log_parts[2:3])
                parts.append(orecv[unit, i, head, :HD].astype(F32))
            top = functools.reduce(jnp.maximum, stats)
            shares = [jnp.exp2(s - top) for s in stats]
            total = functools.reduce(jnp.add, shares)
            video = functools.reduce(jnp.add, [p * s for p, s in zip(parts, shares)]) / total
            video_log = top + jnp.log2(total)
            halves = []
            for half in range(2):
                text_top = textstat[head, half, 0:1, span]
                text_total = textstat[head, half, 1:2, span]
                both = jnp.maximum(video_log, text_top)
                a, b = jnp.exp2(video_log - both), jnp.exp2(text_top - both)
                scale = 1.0 / (a + b * text_total)
                halves.append(video * (a * scale) + textout[head, half, :, span] * (b * scale))
            guided = halves[1] + guidance * (halves[0] - halves[1])
            rows = guided.T.astype(BF16)
            columns = slice(head * HD, (head + 1) * HD)
            abuf[unit, 0, :, columns] = rows[:ROWS]
            asend[unit, 0, :, columns] = rows[:ROWS]
            asend[unit, 1, :, columns] = rows[ROWS:]
        here = pl.ds(group[0] * HD, len(group) * HD)
        there = pl.ds(OWN + group[0] * HD, len(group) * HD)
        swapped[unit] += [
            send(asend.at[unit, 0, :, here], abuf.at[unit, 1, :, here], device(0, 0, 2, 0)),
            send(asend.at[unit, 1, :, here], abuf.at[unit, 1, :, there], device(0, 0, 2, 1)),
            send(asend.at[unit, 1, :, here], abuf.at[unit, 0, :, there], other),
        ]

    def output(unit):
        for copy in swapped[unit]:
            copy.wait_recv()
        return jnp.dot(
            abuf[unit].reshape(UNIT, 2 * OWN), wo[...], preferred_element_type=F32
        ).reshape(2, ROWS, HALF)

    text_copy.wait()
    for head in range(HEADS):
        text_attention(head)
    send_far_kv(3)
    send_far_q(3)
    send_near_q(2)
    def arrived(copies):
        for copy in copies:
            copy.wait_recv()

    every = (0, 1, 2)
    for unit in range(UNITS):
        arrived(far_kv[unit])
    arrived(far_q[3])
    attend(3, every, sends=(every,))
    send_far_q(2)
    arrived(far_q[1])
    attend(1, every, sends=(every,))
    combine(3, every)
    arrived(far_q[2])
    attend(2, every, sends=(every,))
    for copy in wo_copies:
        copy.wait()
    dsend[...] = output(3).astype(BF16)
    cuts = [pl.ds(at, SUM_COLUMNS) for at in range(0, HALF, SUM_COLUMNS)]
    far_sum = [
        (
            send(dsend.at[:, low, cut], drecv.at[0, :, :, cut], up),
            send(dsend.at[:, high, cut], drecv.at[1, :, :, cut], down),
        )
        for cut in cuts
    ]
    combine(1, every)
    arrived(far_q[0])
    attend(0, (0, 1), sends=((0, 1),))
    nsend[0] = output(1).astype(BF16)
    near_sum = [
        send(nsend.at[0, :, low], nrecv.at[0, :, low], down),
        send(nsend.at[0, :, high], nrecv.at[1, :, high], up),
    ]
    combine(2, every)
    attend(0, (2,), sends=((2,),))
    product = output(2)
    for copies, cut in zip(far_sum, cuts):
        arrived(copies)
        columns = slice(cut.start, cut.start + SUM_COLUMNS)
        nsend[1, :, :PART, columns] = (
            product[:, :PART, columns] + drecv[1, :, :, columns].astype(F32)
        ).astype(BF16)
        nsend[1, :, PART:, columns] = (
            product[:, PART:, columns] + drecv[0, :, :, columns].astype(F32)
        ).astype(BF16)
        near_sum += [
            send(nsend.at[1, :, low, cut], nrecv.at[0, :, high, cut], down),
            send(nsend.at[1, :, high, cut], nrecv.at[1, :, low, cut], up),
        ]
    combine(0, (0, 1))
    combine(0, (2,))
    xcols_copy.wait()
    position = index_ref[0]
    sigma_step = sigmas_ref[position + 1] - sigmas_ref[position]
    product = output(0)
    for copy in near_sum:
        copy.wait_recv()
    guided = product + nrecv[0].astype(F32) + nrecv[1].astype(F32)
    for at, half in enumerate((z_hi, 1 - z_hi)):
        rows = pl.ds(pl.multiple_of(half * ROWS, ROWS), ROWS)
        guided_ref[rows] = guided[at].astype(BF16)
        next_ref[rows] = (xcols[rows].astype(F32) + sigma_step * guided[at]).astype(BF16)
    for copy in sent:
        copy.wait_send()


def hand_over(guided_ref, next_ref, guided_out, next_out):
    guided_out[...] = guided_ref[...]
    next_out[...] = next_ref[...]


def per_device(latents, w_qkv, w_out, q_gain, k_gain, text_kv, text_lengths, sigmas, step_index, guidance):
    any_space = pl.BlockSpec(memory_space=pl.ANY)
    vmem = pl.BlockSpec(memory_space=pltpu.VMEM)
    smem = pl.BlockSpec(memory_space=pltpu.SMEM)
    out = jax.ShapeDtypeStruct((2 * ROWS, HALF), BF16)
    guided, latents_after = pl.pallas_call(
        step_kernel,
        name="denoising_step",
        out_shape=(out, out),
        in_specs=[any_space] * 4 + [vmem] * 2 + [smem] * 4,
        out_specs=(vmem, vmem),
        scratch_shapes=[
            pltpu.VMEM((UNITS, 2, ROWS, WIDTH), BF16),
            pltpu.VMEM((WIDTH, 3 * OWN), BF16),
            pltpu.VMEM((2 * OWN, HALF), BF16),
            pltpu.VMEM((2, 2, 256, OWN), BF16),
            pltpu.VMEM((2 * ROWS, HALF), BF16),
            pltpu.VMEM((4, UNITS, HEADS, UNIT, HD), BF16),
            pltpu.VMEM((4, UNITS, 2, HEADS, UNIT, HD), BF16),
            pltpu.VMEM((UNITS, HEADS, UNIT, HD), BF16),
            pltpu.VMEM((HEADS, 2, HD, UNITS * UNIT), F32),
            pltpu.VMEM((HEADS, 2, 8, UNITS * UNIT), F32),
            pltpu.VMEM((UNITS, 3, HEADS, HD + STAT, UNIT), BF16),
            pltpu.VMEM((UNITS, 3, HEADS, HD + STAT, UNIT), BF16),
            pltpu.VMEM((UNITS, HEADS, HD, UNIT), F32),
            pltpu.VMEM((UNITS, 8, UNIT), F32),
            pltpu.VMEM((UNITS, 2, ROWS, OWN), BF16),
            pltpu.VMEM((UNITS, 2, ROWS, 2 * OWN), BF16),
            pltpu.VMEM((2, ROWS, HALF), BF16),
            pltpu.VMEM((2, 2, PART, HALF), BF16),
            pltpu.VMEM((2, 2, ROWS, HALF), BF16),
            pltpu.VMEM((2, 2, ROWS, HALF), BF16),
            pltpu.SemaphoreType.DMA((16,)),
            pltpu.SemaphoreType.DMA((MESSAGES,)),
            pltpu.SemaphoreType.DMA((MESSAGES,)),
        ],
        compiler_params=pltpu.CompilerParams(
            collective_id=0, has_side_effects=True, vmem_limit_bytes=60 * 2**20
        ),
        cost_estimate=pl.CostEstimate(
            flops=12 * 10**9, bytes_accessed=15 * 10**6, transcendentals=14 * 10**6
        ),
    )(
        latents,
        jnp.transpose(w_qkv, (1, 0, 2)),
        w_out,
        text_kv,
        q_gain.reshape(1, HD),
        k_gain.reshape(1, HD),
        text_lengths,
        sigmas,
        step_index,
        guidance,
    )
    return pl.pallas_call(
        hand_over, name="hand_over", out_shape=(out, out), in_specs=[vmem, vmem], out_specs=(vmem, vmem)
    )(guided, latents_after)


def solution(mesh):
    placed = (
        P(("blk", "ulysses"), None),
        P(None, None, "ulysses"),
        P("ulysses", None),
        P(),
        P(),
        P(None, None, None, "ulysses"),
        P(),
        P(),
        P(),
        P(),
    )
    return jax.shard_map(
        per_device,
        mesh=mesh,
        in_specs=placed,
        out_specs=(P(("blk", "ulysses"), "cfg"), P(("blk", "ulysses"), "cfg")),
        check_vma=False,
    )
```

```python
import functools
import math

import jax
import jax.numpy as jnp
from jax import lax
from jax.experimental import pallas as pl
from jax.experimental.pallas import tpu as pltpu
from jax.sharding import PartitionSpec as P

HD = 128
EPS = 1e-06
LOG2E = math.log2(math.e)
SCORE = LOG2E / math.sqrt(HD)
MESH = pl.DeviceIdType.MESH
NT = (((1,), (1,)), ((), ()))
TN = (((0,), (0,)), ((), ()))
F32 = jnp.float32
BF16 = jnp.bfloat16

HEADS = 3
ROWS = 64
PART = ROWS // 2
UNITS = 4
UNIT = 2 * ROWS
QUERIES = 4 * UNIT
WIDTH = 3072
HALF = WIDTH // 2
OWN = HEADS * HD
STAT = 16
SUM_COLUMNS = 768
MESSAGES = 128


def place():
    blk = lax.axis_index("blk")
    z_hi = lax.axis_index("cfg")
    core = lax.rem(blk, 2)
    x = lax.rem(lax.div(blk, 2), 4)
    z = z_hi * 2 + lax.div(blk, 8)
    return x, lax.axis_index("ulysses"), z, core, z_hi


def step_kernel(
    x_hbm,
    wqkv_hbm,
    wout_hbm,
    text_hbm,
    qgain_ref,
    kgain_ref,
    lengths_ref,
    sigmas_ref,
    index_ref,
    guidance_ref,
    guided_ref,
    next_ref,
    xg,
    wq,
    wo,
    text,
    xcols,
    qs,
    kv,
    qtext,
    textout,
    textstat,
    osend,
    orecv,
    oown,
    lown,
    asend,
    abuf,
    dsend,
    drecv,
    nsend,
    nrecv,
    local_sem,
    send_sem,
    recv_sem,
):
    x, y, z, core, z_hi = place()

    def device(dx, dy, dz, dc):
        tx = lax.rem(x + dx + 4, 4)
        ty = lax.rem(y + dy + 4, 4)
        tz = lax.rem(z + dz + 4, 4)
        tc = lax.rem(core + dc, 2)
        return (lax.div(tz, 2), lax.rem(tz, 2) * 8 + tx * 2 + tc, ty)

    def key_device(d):
        return device((1 - core) * d, 0, core * d, 0)

    def query_device(d):
        return device(core * d, 0, (1 - core) * d, 0)

    locals_started = []

    def local(src, dst):
        copy = pltpu.make_async_copy(src, dst, local_sem.at[len(locals_started)])
        copy.start()
        locals_started.append(copy)
        return copy

    own_rows = x_hbm.at[pl.ds(pl.multiple_of(z_hi * ROWS, ROWS), ROWS)]
    own_copy = local(own_rows, xg.at[0, 0])
    own_col = pl.multiple_of(core * OWN, OWN)
    w_copies = [
        local(wqkv_hbm.at[which, :, pl.ds(own_col, OWN)], wq.at[:, pl.ds(at * OWN, OWN)])
        for at, which in enumerate((1, 2, 0))
    ]
    text_copy = local(text_hbm.at[:, :, :, pl.ds(own_col, OWN)], text)
    columns_here = pl.ds(pl.multiple_of(z_hi * HALF, HALF), HALF)
    wo_copies = [
        local(wout_hbm.at[pl.ds(pl.multiple_of(c * OWN, OWN), OWN), columns_here], wo.at[pl.ds(at * OWN, OWN)])
        for at, c in enumerate((core, 1 - core))
    ]
    xcols_copy = local(x_hbm.at[:, columns_here], xcols)

    barrier = pltpu.get_barrier_semaphore()
    greeted = [
        (0, 1, 0, 0),
        (0, -1, 0, 0),
        (0, 0, 0, 1),
        (1, 0, 0, 0),
        (-1, 0, 0, 0),
        (2, 0, 0, 0),
        (0, 0, 1, 0),
        (0, 0, -1, 0),
        (0, 0, 2, 0),
        (0, 0, 2, 1),
    ]
    for offset in greeted:
        pl.semaphore_signal(barrier, inc=1, device_id=device(*offset), device_id_type=MESH)
    pl.semaphore_wait(barrier, len(greeted))

    sent = []

    def send(src, dst, to):
        number = len(sent)
        copy = pltpu.make_async_remote_copy(
            src_ref=src,
            dst_ref=dst,
            send_sem=send_sem.at[number],
            recv_sem=recv_sem.at[number],
            device_id=to,
            device_id_type=MESH,
        )
        copy.start()
        sent.append(copy)
        return copy

    up, down, other = device(0, 1, 0, 0), device(0, -1, 0, 0), device(0, 0, 0, 1)
    low, high = pl.ds(0, PART), pl.ds(PART, PART)

    def own_part(part):
        return x_hbm.at[pl.ds(pl.multiple_of(z_hi * ROWS + part * PART, PART), PART)]

    up_first = send(own_part(0), xg.at[1, 0, low], up)
    down_first = send(own_part(1), xg.at[1, 0, high], down)
    across = [send(own_rows, xg.at[0, 1], other)]
    up_second = send(own_part(1), xg.at[2, 0, low], up)
    down_second = send(own_part(0), xg.at[2, 0, high], down)

    def normed(value, gain):
        mean_square = jnp.mean(value * value, axis=1, keepdims=True)
        return value * lax.rsqrt(mean_square + EPS) * gain

    def project(unit):
        product = jnp.dot(
            xg[unit].reshape(UNIT, WIDTH), wq[...], preferred_element_type=F32
        )
        for head in range(HEADS):
            at = head * HD
            key = normed(product[:, at : at + HD], kgain_ref[...])
            kv[0, unit, 0, head] = key.astype(BF16)
            kv[0, unit, 1, head] = product[:, OWN + at : OWN + at + HD].T.astype(BF16)
            query = normed(product[:, 2 * OWN + at : 2 * OWN + at + HD], qgain_ref[...])
            qtext[unit, head] = query.astype(BF16)
            qs[0, unit, head] = (query * SCORE).astype(BF16)

    near_kv, near_q, far_kv, far_q = {}, {}, {}, {}

    def send_near_kv(unit):
        near_kv[unit] = [
            send(kv.at[0, unit], kv.at[1, unit], key_device(1)),
            send(kv.at[0, unit], kv.at[2, unit], key_device(-1)),
        ]

    def send_near_q(unit):
        near_q[unit] = [
            send(qs.at[0, unit], qs.at[1, unit], query_device(1)),
            send(qs.at[0, unit], qs.at[2, unit], query_device(-1)),
        ]

    def send_far_kv(unit):
        for copy in near_kv[unit]:
            copy.wait_recv()
        far_kv[unit] = [
            send(kv.at[1, unit, 0], kv.at[3, unit, 0], key_device(1)),
            send(kv.at[2, unit, 1], kv.at[3, unit, 1], key_device(-1)),
        ]

    def send_far_q(unit):
        for copy in near_q[unit]:
            copy.wait_recv()
        first, second = pl.ds(0, UNIT // 2), pl.ds(UNIT // 2, UNIT // 2)
        far_q[unit] = [
            send(qs.at[1, unit, :, first], qs.at[3, unit, :, first], query_device(1)),
            send(qs.at[2, unit, :, second], qs.at[3, unit, :, second], query_device(-1)),
        ]

    for copy in w_copies:
        copy.wait()
    own_copy.wait()
    across[0].wait_recv()
    project(0)
    send_near_kv(0)
    send_near_q(0)
    up_first.wait_recv()
    far_up = send(xg.at[1, 0, low], xg.at[3, 0, low], up)
    down_first.wait_recv()
    far_down = send(xg.at[1, 0, high], xg.at[3, 0, high], down)
    across.append(send(xg.at[1, 0], xg.at[1, 1], other))
    across[1].wait_recv()
    project(1)
    send_near_kv(1)
    send_near_q(1)
    send_far_kv(0)
    send_far_q(0)
    up_second.wait_recv()
    down_second.wait_recv()
    across.append(send(xg.at[2, 0], xg.at[2, 1], other))
    across[2].wait_recv()
    project(2)
    send_near_kv(2)
    send_far_kv(1)
    send_far_q(1)
    far_up.wait_recv()
    far_down.wait_recv()
    across.append(send(xg.at[3, 0], xg.at[3, 1], other))
    across[3].wait_recv()
    project(3)
    send_near_kv(3)
    send_near_q(3)
    send_far_kv(2)

    def text_attention(head):
        columns = slice(head * HD, (head + 1) * HD)
        queries = qtext[:, head].reshape(UNITS * UNIT, HD)
        for half in range(2):
            scores = (
                lax.dot_general(text[half, 0, :, columns], queries, NT, preferred_element_type=F32)
                * SCORE
            )
            valid = lax.broadcasted_iota(jnp.int32, scores.shape, 0) < lengths_ref[half]
            scores = jnp.where(valid, scores, -jnp.inf)
            top = jnp.max(scores, axis=0, keepdims=True)
            weights = jnp.exp2(scores - top)
            total = jnp.sum(weights, axis=0, keepdims=True)
            textout[head, half] = lax.dot_general(
                text[half, 1, :, columns], weights.astype(BF16), TN, preferred_element_type=F32
            )
            textstat[head, half, 0:1] = top
            textstat[head, half, 1:2] = total

    back = {}

    def attend(unit, heads, sends):
        steps = [(head, pair) for head in heads for pair in range(2)]
        scores_of = {}

        def score(head, pair):
            keys = kv[2 * pair : 2 * pair + 2, :, 0, head].reshape(2 * UNITS * UNIT, HD)
            queries = qs[:, unit, head].reshape(QUERIES, HD)
            return lax.dot_general(keys, queries, NT, preferred_element_type=F32)

        scores_of[steps[0]] = score(*steps[0])
        for n, (head, pair) in enumerate(steps):
            if n + 1 < len(steps):
                scores_of[steps[n + 1]] = score(*steps[n + 1])
            scores = scores_of.pop((head, pair))
            new_top = jnp.max(scores, axis=0, keepdims=True)
            if pair:
                new_top = jnp.maximum(new_top, top)
            weights = jnp.exp2(scores - new_top)
            part_total = jnp.sum(weights, axis=0, keepdims=True)
            values = jnp.concatenate(
                [kv[slot, u, 1, head] for slot in (2 * pair, 2 * pair + 1) for u in range(UNITS)], axis=1
            )
            product = jnp.dot(values, weights.astype(BF16), preferred_element_type=F32)
            if pair:
                shrink = jnp.exp2(top - new_top)
                part_total = total * shrink + part_total
                product = weighted * shrink + product
            top, total, weighted = new_top, part_total, product
            if not pair:
                continue
            result = weighted / total
            log_total = top + jnp.log2(total)
            row = lax.broadcasted_iota(jnp.int32, (STAT, UNIT), 0)
            for slot in range(4):
                part = result[:, slot * UNIT : (slot + 1) * UNIT]
                stat = log_total[:, slot * UNIT : (slot + 1) * UNIT]
                if slot == 0:
                    oown[unit, head] = part
                    lown[unit, head : head + 1] = stat
                else:
                    first = stat.astype(BF16).astype(F32)
                    second = (stat - first).astype(BF16).astype(F32)
                    third = stat - first - second
                    osend[unit, slot - 1, head, :HD] = part.astype(BF16)
                    osend[unit, slot - 1, head, HD:] = jnp.where(
                        row == 0, first, jnp.where(row == 1, second, third)
                    ).astype(BF16)
            for group in sends:
                if head == group[-1]:
                    send_back(unit, group)

    def send_back(unit, group):
        span = pl.ds(group[0], len(group))
        back[unit, group] = [
            send(osend.at[unit, slot - 1, span], orecv.at[unit, lands - 1, span], query_device(d))
            for slot, d, lands in ((3, 2, 3), (1, -1, 2), (2, 1, 1))
        ]

    guidance = guidance_ref[0]
    swapped = {unit: [] for unit in range(UNITS)}

    def combine(unit, group):
        for copy in back[unit, group]:
            copy.wait_recv()
        span = slice(unit * UNIT, (unit + 1) * UNIT)
        for head in group:
            stats = [lown[unit, head : head + 1]]
            parts = [oown[unit, head]]
            for i in range(3):
                log_parts = orecv[unit, i, head, HD:].astype(F32)
                stats.append(log_parts[0:1] + log_parts[1:2] + log_parts[2:3])
                parts.append(orecv[unit, i, head, :HD].astype(F32))
            top = functools.reduce(jnp.maximum, stats)
            shares = [jnp.exp2(s - top) for s in stats]
            total = functools.reduce(jnp.add, shares)
            video = functools.reduce(jnp.add, [p * s for p, s in zip(parts, shares)]) / total
            video_log = top + jnp.log2(total)
            halves = []
            for half in range(2):
                text_top = textstat[head, half, 0:1, span]
                text_total = textstat[head, half, 1:2, span]
                both = jnp.maximum(video_log, text_top)
                a, b = jnp.exp2(video_log - both), jnp.exp2(text_top - both)
                scale = 1.0 / (a + b * text_total)
                halves.append(video * (a * scale) + textout[head, half, :, span] * (b * scale))
            guided = halves[1] + guidance * (halves[0] - halves[1])
            rows = guided.T.astype(BF16)
            columns = slice(head * HD, (head + 1) * HD)
            abuf[unit, 0, :, columns] = rows[:ROWS]
            asend[unit, 0, :, columns] = rows[:ROWS]
            asend[unit, 1, :, columns] = rows[ROWS:]
        here = pl.ds(group[0] * HD, len(group) * HD)
        there = pl.ds(OWN + group[0] * HD, len(group) * HD)
        swapped[unit] += [
            send(asend.at[unit, 0, :, here], abuf.at[unit, 1, :, here], device(0, 0, 2, 0)),
            send(asend.at[unit, 1, :, here], abuf.at[unit, 1, :, there], device(0, 0, 2, 1)),
            send(asend.at[unit, 1, :, here], abuf.at[unit, 0, :, there], other),
        ]

    def output(unit):
        for copy in swapped[unit]:
            copy.wait_recv()
        return jnp.dot(
            abuf[unit].reshape(UNIT, 2 * OWN), wo[...], preferred_element_type=F32
        ).reshape(2, ROWS, HALF)

    text_copy.wait()
    for head in range(HEADS):
        text_attention(head)
    send_far_kv(3)
    send_far_q(3)
    def arrived(copies):
        for copy in copies:
            copy.wait_recv()

    every = (0, 1, 2)
    for unit in range(UNITS):
        arrived(far_kv[unit])
    arrived(far_q[3])
    send_near_q(2)
    attend(3, every, sends=((0, 1), (2,)))
    send_far_q(2)
    arrived(far_q[1])
    attend(1, (0, 1), sends=())
    combine(3, (0, 1))
    combine(3, (2,))
    attend(1, (2,), sends=())
    send_back(1, every)
    arrived(far_q[2])
    attend(2, every, sends=(every,))
    for copy in wo_copies:
        copy.wait()
    dsend[...] = output(3).astype(BF16)
    cuts = [pl.ds(at, SUM_COLUMNS) for at in range(0, HALF, SUM_COLUMNS)]
    far_sum = [
        (
            send(dsend.at[:, low, cut], drecv.at[0, :, :, cut], up),
            send(dsend.at[:, high, cut], drecv.at[1, :, :, cut], down),
        )
        for cut in cuts
    ]
    combine(1, every)
    arrived(far_q[0])
    attend(0, (0, 1), sends=((0, 1),))
    combine(2, every)
    nsend[0] = output(1).astype(BF16)
    near_sum = [
        send(nsend.at[0, :, low], nrecv.at[0, :, low], down),
        send(nsend.at[0, :, high], nrecv.at[1, :, high], up),
    ]
    attend(0, (2,), sends=((2,),))
    combine(0, (0, 1))
    product = output(2)
    for copies, cut in zip(far_sum, cuts):
        arrived(copies)
        columns = slice(cut.start, cut.start + SUM_COLUMNS)
        nsend[1, :, :PART, columns] = (
            product[:, :PART, columns] + drecv[1, :, :, columns].astype(F32)
        ).astype(BF16)
        nsend[1, :, PART:, columns] = (
            product[:, PART:, columns] + drecv[0, :, :, columns].astype(F32)
        ).astype(BF16)
        near_sum += [
            send(nsend.at[1, :, low, cut], nrecv.at[0, :, high, cut], down),
            send(nsend.at[1, :, high, cut], nrecv.at[1, :, low, cut], up),
        ]
    combine(0, (2,))
    xcols_copy.wait()
    position = index_ref[0]
    sigma_step = sigmas_ref[position + 1] - sigmas_ref[position]
    product = output(0)
    for copy in near_sum:
        copy.wait_recv()
    guided = product + nrecv[0].astype(F32) + nrecv[1].astype(F32)
    for at, half in enumerate((z_hi, 1 - z_hi)):
        rows = pl.ds(pl.multiple_of(half * ROWS, ROWS), ROWS)
        guided_ref[rows] = guided[at].astype(BF16)
        next_ref[rows] = (xcols[rows].astype(F32) + sigma_step * guided[at]).astype(BF16)
    for copy in sent:
        copy.wait_send()


def hand_over(guided_ref, next_ref, guided_out, next_out):
    guided_out[...] = guided_ref[...]
    next_out[...] = next_ref[...]


def per_device(latents, w_qkv, w_out, q_gain, k_gain, text_kv, text_lengths, sigmas, step_index, guidance):
    any_space = pl.BlockSpec(memory_space=pl.ANY)
    vmem = pl.BlockSpec(memory_space=pltpu.VMEM)
    smem = pl.BlockSpec(memory_space=pltpu.SMEM)
    out = jax.ShapeDtypeStruct((2 * ROWS, HALF), BF16)
    guided, latents_after = pl.pallas_call(
        step_kernel,
        name="denoising_step",
        out_shape=(out, out),
        in_specs=[any_space] * 4 + [vmem] * 2 + [smem] * 4,
        out_specs=(vmem, vmem),
        scratch_shapes=[
            pltpu.VMEM((UNITS, 2, ROWS, WIDTH), BF16),
            pltpu.VMEM((WIDTH, 3 * OWN), BF16),
            pltpu.VMEM((2 * OWN, HALF), BF16),
            pltpu.VMEM((2, 2, 256, OWN), BF16),
            pltpu.VMEM((2 * ROWS, HALF), BF16),
            pltpu.VMEM((4, UNITS, HEADS, UNIT, HD), BF16),
            pltpu.VMEM((4, UNITS, 2, HEADS, UNIT, HD), BF16),
            pltpu.VMEM((UNITS, HEADS, UNIT, HD), BF16),
            pltpu.VMEM((HEADS, 2, HD, UNITS * UNIT), F32),
            pltpu.VMEM((HEADS, 2, 8, UNITS * UNIT), F32),
            pltpu.VMEM((UNITS, 3, HEADS, HD + STAT, UNIT), BF16),
            pltpu.VMEM((UNITS, 3, HEADS, HD + STAT, UNIT), BF16),
            pltpu.VMEM((UNITS, HEADS, HD, UNIT), F32),
            pltpu.VMEM((UNITS, 8, UNIT), F32),
            pltpu.VMEM((UNITS, 2, ROWS, OWN), BF16),
            pltpu.VMEM((UNITS, 2, ROWS, 2 * OWN), BF16),
            pltpu.VMEM((2, ROWS, HALF), BF16),
            pltpu.VMEM((2, 2, PART, HALF), BF16),
            pltpu.VMEM((2, 2, ROWS, HALF), BF16),
            pltpu.VMEM((2, 2, ROWS, HALF), BF16),
            pltpu.SemaphoreType.DMA((16,)),
            pltpu.SemaphoreType.DMA((MESSAGES,)),
            pltpu.SemaphoreType.DMA((MESSAGES,)),
        ],
        compiler_params=pltpu.CompilerParams(
            collective_id=0, has_side_effects=True, vmem_limit_bytes=60 * 2**20
        ),
        cost_estimate=pl.CostEstimate(
            flops=12 * 10**9, bytes_accessed=15 * 10**6, transcendentals=14 * 10**6
        ),
    )(
        latents,
        jnp.transpose(w_qkv, (1, 0, 2)),
        w_out,
        text_kv,
        q_gain.reshape(1, HD),
        k_gain.reshape(1, HD),
        text_lengths,
        sigmas,
        step_index,
        guidance,
    )
    return pl.pallas_call(
        hand_over,
        name="hand_over",
        out_shape=(out, out),
        in_specs=[vmem, vmem],
        out_specs=(vmem, vmem),
    )(guided, latents_after)


def solution(mesh):
    placed = (
        P(("blk", "ulysses"), None),
        P(None, None, "ulysses"),
        P("ulysses", None),
        P(),
        P(),
        P(None, None, None, "ulysses"),
        P(),
        P(),
        P(),
        P(),
    )
    return jax.shard_map(
        per_device,
        mesh=mesh,
        in_specs=placed,
        out_specs=(P(("blk", "ulysses"), "cfg"), P(("blk", "ulysses"), "cfg")),
        check_vma=False,
    )
```

```python
import functools
import math

import jax
import jax.numpy as jnp
from jax import lax
from jax.experimental import pallas as pl
from jax.experimental.pallas import tpu as pltpu
from jax.sharding import PartitionSpec as P

HD = 128
EPS = 1e-06
LOG2E = math.log2(math.e)
SCORE = LOG2E / math.sqrt(HD)
MESH = pl.DeviceIdType.MESH
NT = (((1,), (1,)), ((), ()))
TN = (((0,), (0,)), ((), ()))
F32 = jnp.float32
BF16 = jnp.bfloat16

HEADS = 3
ROWS = 64
PART = ROWS // 2
UNITS = 4
UNIT = 2 * ROWS
QUERIES = 4 * UNIT
WIDTH = 3072
HALF = WIDTH // 2
OWN = HEADS * HD
STAT = 16
SUM_COLUMNS = 768
MESSAGES = 128


def place():
    blk = lax.axis_index("blk")
    z_hi = lax.axis_index("cfg")
    core = lax.rem(blk, 2)
    x = lax.rem(lax.div(blk, 2), 4)
    z = z_hi * 2 + lax.div(blk, 8)
    return x, lax.axis_index("ulysses"), z, core, z_hi


def step_kernel(
    x_hbm,
    wqkv_hbm,
    wout_hbm,
    text_hbm,
    qgain_ref,
    kgain_ref,
    lengths_ref,
    sigmas_ref,
    index_ref,
    guidance_ref,
    guided_ref,
    next_ref,
    xg,
    wq,
    wo,
    text,
    xcols,
    qs,
    kv,
    qtext,
    textout,
    textstat,
    osend,
    orecv,
    oown,
    lown,
    kept,
    keptstat,
    asend,
    abuf,
    dsend,
    drecv,
    nsend,
    nrecv,
    local_sem,
    send_sem,
    recv_sem,
):
    x, y, z, core, z_hi = place()

    def device(dx, dy, dz, dc):
        tx = lax.rem(x + dx + 4, 4)
        ty = lax.rem(y + dy + 4, 4)
        tz = lax.rem(z + dz + 4, 4)
        tc = lax.rem(core + dc, 2)
        return (lax.div(tz, 2), lax.rem(tz, 2) * 8 + tx * 2 + tc, ty)

    def key_device(d):
        return device((1 - core) * d, 0, core * d, 0)

    def query_device(d):
        return device(core * d, 0, (1 - core) * d, 0)

    locals_started = []

    def local(src, dst):
        copy = pltpu.make_async_copy(src, dst, local_sem.at[len(locals_started)])
        copy.start()
        locals_started.append(copy)
        return copy

    own_rows = x_hbm.at[pl.ds(pl.multiple_of(z_hi * ROWS, ROWS), ROWS)]
    own_copy = local(own_rows, xg.at[0, 0])
    own_col = pl.multiple_of(core * OWN, OWN)
    w_copies = [
        local(wqkv_hbm.at[which, :, pl.ds(own_col, OWN)], wq.at[:, pl.ds(at * OWN, OWN)])
        for at, which in enumerate((1, 2, 0))
    ]
    text_copy = local(text_hbm.at[:, :, :, pl.ds(own_col, OWN)], text)
    columns_here = pl.ds(pl.multiple_of(z_hi * HALF, HALF), HALF)
    wo_copies = [
        local(wout_hbm.at[pl.ds(pl.multiple_of(c * OWN, OWN), OWN), columns_here], wo.at[pl.ds(at * OWN, OWN)])
        for at, c in enumerate((core, 1 - core))
    ]
    xcols_copy = local(x_hbm.at[:, columns_here], xcols)

    barrier = pltpu.get_barrier_semaphore()
    greeted = [
        (0, 1, 0, 0),
        (0, -1, 0, 0),
        (0, 0, 0, 1),
        (1, 0, 0, 0),
        (-1, 0, 0, 0),
        (2, 0, 0, 0),
        (0, 0, 1, 0),
        (0, 0, -1, 0),
        (0, 0, 2, 0),
        (0, 0, 2, 1),
    ]
    for offset in greeted:
        pl.semaphore_signal(barrier, inc=1, device_id=device(*offset), device_id_type=MESH)
    pl.semaphore_wait(barrier, len(greeted))

    sent = []

    def send(src, dst, to):
        number = len(sent)
        copy = pltpu.make_async_remote_copy(
            src_ref=src,
            dst_ref=dst,
            send_sem=send_sem.at[number],
            recv_sem=recv_sem.at[number],
            device_id=to,
            device_id_type=MESH,
        )
        copy.start()
        sent.append(copy)
        return copy

    up, down, other = device(0, 1, 0, 0), device(0, -1, 0, 0), device(0, 0, 0, 1)
    low, high = pl.ds(0, PART), pl.ds(PART, PART)

    def own_part(part):
        return x_hbm.at[pl.ds(pl.multiple_of(z_hi * ROWS + part * PART, PART), PART)]

    up_first = send(own_part(0), xg.at[1, 0, low], up)
    down_first = send(own_part(1), xg.at[1, 0, high], down)
    across = [send(own_rows, xg.at[0, 1], other)]
    up_second = send(own_part(1), xg.at[2, 0, low], up)
    down_second = send(own_part(0), xg.at[2, 0, high], down)

    def normed(value, gain):
        mean_square = jnp.mean(value * value, axis=1, keepdims=True)
        return value * lax.rsqrt(mean_square + EPS) * gain

    def project(unit):
        product = jnp.dot(
            xg[unit].reshape(UNIT, WIDTH), wq[...], preferred_element_type=F32
        )
        for head in range(HEADS):
            at = head * HD
            key = normed(product[:, at : at + HD], kgain_ref[...])
            kv[0, unit, 0, head] = key.astype(BF16)
            kv[0, unit, 1, head] = product[:, OWN + at : OWN + at + HD].T.astype(BF16)
            query = normed(product[:, 2 * OWN + at : 2 * OWN + at + HD], qgain_ref[...])
            qtext[unit, head] = query.astype(BF16)
            qs[0, unit, head] = (query * SCORE).astype(BF16)

    near_kv, near_q, far_kv, far_q = {}, {}, {}, {}

    def send_near_kv(unit):
        near_kv[unit] = [
            send(kv.at[0, unit], kv.at[1, unit], key_device(1)),
            send(kv.at[0, unit], kv.at[2, unit], key_device(-1)),
        ]

    def send_near_q(unit):
        near_q[unit] = [
            send(qs.at[0, unit], qs.at[1, unit], query_device(1)),
            send(qs.at[0, unit], qs.at[2, unit], query_device(-1)),
        ]

    def send_far_kv(unit):
        for copy in near_kv[unit]:
            copy.wait_recv()
        far_kv[unit] = [
            send(kv.at[1, unit, 0], kv.at[3, unit, 0], key_device(1)),
            send(kv.at[2, unit, 1], kv.at[3, unit, 1], key_device(-1)),
        ]

    def send_far_q(unit):
        for copy in near_q[unit]:
            copy.wait_recv()
        first, second = pl.ds(0, UNIT // 2), pl.ds(UNIT // 2, UNIT // 2)
        far_q[unit] = [
            send(qs.at[1, unit, :, first], qs.at[3, unit, :, first], query_device(1)),
            send(qs.at[2, unit, :, second], qs.at[3, unit, :, second], query_device(-1)),
        ]

    for copy in w_copies:
        copy.wait()
    own_copy.wait()
    across[0].wait_recv()
    project(0)
    send_near_kv(0)
    send_near_q(0)
    up_first.wait_recv()
    far_up = send(xg.at[1, 0, low], xg.at[3, 0, low], up)
    down_first.wait_recv()
    far_down = send(xg.at[1, 0, high], xg.at[3, 0, high], down)
    across.append(send(xg.at[1, 0], xg.at[1, 1], other))
    across[1].wait_recv()
    project(1)
    send_near_kv(1)
    send_near_q(1)
    send_far_kv(0)
    send_far_q(0)
    up_second.wait_recv()
    down_second.wait_recv()
    across.append(send(xg.at[2, 0], xg.at[2, 1], other))
    across[2].wait_recv()
    project(2)
    send_near_kv(2)
    send_far_kv(1)
    send_far_q(1)
    far_up.wait_recv()
    far_down.wait_recv()
    across.append(send(xg.at[3, 0], xg.at[3, 1], other))
    across[3].wait_recv()
    project(3)
    send_near_kv(3)
    send_near_q(3)
    send_far_kv(2)

    def text_attention(head):
        columns = slice(head * HD, (head + 1) * HD)
        queries = qtext[:, head].reshape(UNITS * UNIT, HD)
        for half in range(2):
            scores = (
                lax.dot_general(text[half, 0, :, columns], queries, NT, preferred_element_type=F32)
                * SCORE
            )
            valid = lax.broadcasted_iota(jnp.int32, scores.shape, 0) < lengths_ref[half]
            scores = jnp.where(valid, scores, -jnp.inf)
            top = jnp.max(scores, axis=0, keepdims=True)
            weights = jnp.exp2(scores - top)
            total = jnp.sum(weights, axis=0, keepdims=True)
            textout[head, half] = lax.dot_general(
                text[half, 1, :, columns], weights.astype(BF16), TN, preferred_element_type=F32
            )
            textstat[head, half, 0:1] = top
            textstat[head, half, 1:2] = total

    back = {}

    def attend(unit, heads, sends=(), pairs=(0, 1)):
        steps = [(head, pair) for head in heads for pair in pairs]
        scores_of = {}

        def score(head, pair):
            keys = kv[2 * pair : 2 * pair + 2, :, 0, head].reshape(2 * UNITS * UNIT, HD)
            queries = qs[:, unit, head].reshape(QUERIES, HD)
            return lax.dot_general(keys, queries, NT, preferred_element_type=F32)

        scores_of[steps[0]] = score(*steps[0])
        for n, (head, pair) in enumerate(steps):
            if n + 1 < len(steps):
                scores_of[steps[n + 1]] = score(*steps[n + 1])
            scores = scores_of.pop((head, pair))
            if pairs == (1,):
                top, total, weighted = keptstat[head, 0:1], keptstat[head, 1:2], kept[head]
            new_top = jnp.max(scores, axis=0, keepdims=True)
            if pair:
                new_top = jnp.maximum(new_top, top)
            weights = jnp.exp2(scores - new_top)
            part_total = jnp.sum(weights, axis=0, keepdims=True)
            values = jnp.concatenate(
                [kv[slot, u, 1, head] for slot in (2 * pair, 2 * pair + 1) for u in range(UNITS)], axis=1
            )
            product = jnp.dot(values, weights.astype(BF16), preferred_element_type=F32)
            if pair:
                shrink = jnp.exp2(top - new_top)
                part_total = total * shrink + part_total
                product = weighted * shrink + product
            top, total, weighted = new_top, part_total, product
            if pairs == (0,):
                keptstat[head, 0:1], keptstat[head, 1:2], kept[head] = top, total, weighted
            if not pair:
                continue
            result = weighted / total
            log_total = top + jnp.log2(total)
            row = lax.broadcasted_iota(jnp.int32, (STAT, UNIT), 0)
            for slot in range(4):
                part = result[:, slot * UNIT : (slot + 1) * UNIT]
                stat = log_total[:, slot * UNIT : (slot + 1) * UNIT]
                if slot == 0:
                    oown[unit, head] = part
                    lown[unit, head : head + 1] = stat
                else:
                    first = stat.astype(BF16).astype(F32)
                    second = (stat - first).astype(BF16).astype(F32)
                    third = stat - first - second
                    osend[unit, slot - 1, head, :HD] = part.astype(BF16)
                    osend[unit, slot - 1, head, HD:] = jnp.where(
                        row == 0, first, jnp.where(row == 1, second, third)
                    ).astype(BF16)
            for group in sends:
                if head == group[-1]:
                    send_back(unit, group)

    def send_back(unit, group):
        span = pl.ds(group[0], len(group))
        back[unit, group] = [
            send(osend.at[unit, slot - 1, span], orecv.at[unit, lands - 1, span], query_device(d))
            for slot, d, lands in ((3, 2, 3), (1, -1, 2), (2, 1, 1))
        ]

    guidance = guidance_ref[0]
    swapped = {unit: [] for unit in range(UNITS)}

    def combine(unit, group):
        for copy in back[unit, group]:
            copy.wait_recv()
        span = slice(unit * UNIT, (unit + 1) * UNIT)
        for head in group:
            stats = [lown[unit, head : head + 1]]
            parts = [oown[unit, head]]
            for i in range(3):
                log_parts = orecv[unit, i, head, HD:].astype(F32)
                stats.append(log_parts[0:1] + log_parts[1:2] + log_parts[2:3])
                parts.append(orecv[unit, i, head, :HD].astype(F32))
            top = functools.reduce(jnp.maximum, stats)
            shares = [jnp.exp2(s - top) for s in stats]
            total = functools.reduce(jnp.add, shares)
            video = functools.reduce(jnp.add, [p * s for p, s in zip(parts, shares)]) / total
            video_log = top + jnp.log2(total)
            halves = []
            for half in range(2):
                text_top = textstat[head, half, 0:1, span]
                text_total = textstat[head, half, 1:2, span]
                both = jnp.maximum(video_log, text_top)
                a, b = jnp.exp2(video_log - both), jnp.exp2(text_top - both)
                scale = 1.0 / (a + b * text_total)
                halves.append(video * (a * scale) + textout[head, half, :, span] * (b * scale))
            guided = halves[1] + guidance * (halves[0] - halves[1])
            rows = guided.T.astype(BF16)
            columns = slice(head * HD, (head + 1) * HD)
            abuf[unit, 0, :, columns] = rows[:ROWS]
            asend[unit, 0, :, columns] = rows[:ROWS]
            asend[unit, 1, :, columns] = rows[ROWS:]
        here = pl.ds(group[0] * HD, len(group) * HD)
        there = pl.ds(OWN + group[0] * HD, len(group) * HD)
        swapped[unit] += [
            send(asend.at[unit, 0, :, here], abuf.at[unit, 1, :, here], device(0, 0, 2, 0)),
            send(asend.at[unit, 1, :, here], abuf.at[unit, 1, :, there], device(0, 0, 2, 1)),
            send(asend.at[unit, 1, :, here], abuf.at[unit, 0, :, there], other),
        ]

    def output(unit):
        for copy in swapped[unit]:
            copy.wait_recv()
        return jnp.dot(
            abuf[unit].reshape(UNIT, 2 * OWN), wo[...], preferred_element_type=F32
        ).reshape(2, ROWS, HALF)

    text_copy.wait()
    for head in range(HEADS):
        text_attention(head)
    send_far_kv(3)
    send_far_q(3)
    def arrived(copies):
        for copy in copies:
            copy.wait_recv()

    every = (0, 1, 2)
    arrived(far_q[1])
    attend(1, every, pairs=(0,))
    for unit in range(UNITS):
        arrived(far_kv[unit])
    arrived(far_q[3])
    send_near_q(2)
    attend(3, every, sends=((0, 1), (2,)))
    send_far_q(2)
    attend(1, every, sends=(every,), pairs=(1,))
    combine(3, (0, 1))
    combine(3, (2,))
    arrived(far_q[2])
    attend(2, every, sends=(every,))
    for copy in wo_copies:
        copy.wait()
    dsend[...] = output(3).astype(BF16)
    cuts = [pl.ds(at, SUM_COLUMNS) for at in range(0, HALF, SUM_COLUMNS)]
    far_sum = [
        (
            send(dsend.at[:, low, cut], drecv.at[0, :, :, cut], up),
            send(dsend.at[:, high, cut], drecv.at[1, :, :, cut], down),
        )
        for cut in cuts
    ]
    combine(1, every)
    arrived(far_q[0])
    attend(0, (0, 1), sends=((0, 1),))
    combine(2, every)
    nsend[0] = output(1).astype(BF16)
    near_sum = [
        send(nsend.at[0, :, low], nrecv.at[0, :, low], down),
        send(nsend.at[0, :, high], nrecv.at[1, :, high], up),
    ]
    attend(0, (2,), sends=((2,),))
    combine(0, (0, 1))
    product = output(2)
    for copies, cut in zip(far_sum, cuts):
        arrived(copies)
        columns = slice(cut.start, cut.start + SUM_COLUMNS)
        nsend[1, :, :PART, columns] = (
            product[:, :PART, columns] + drecv[1, :, :, columns].astype(F32)
        ).astype(BF16)
        nsend[1, :, PART:, columns] = (
            product[:, PART:, columns] + drecv[0, :, :, columns].astype(F32)
        ).astype(BF16)
        near_sum += [
            send(nsend.at[1, :, low, cut], nrecv.at[0, :, high, cut], down),
            send(nsend.at[1, :, high, cut], nrecv.at[1, :, low, cut], up),
        ]
    combine(0, (2,))
    xcols_copy.wait()
    position = index_ref[0]
    sigma_step = sigmas_ref[position + 1] - sigmas_ref[position]
    product = output(0)
    for copy in near_sum:
        copy.wait_recv()
    guided = product + nrecv[0].astype(F32) + nrecv[1].astype(F32)
    for at, half in enumerate((z_hi, 1 - z_hi)):
        rows = pl.ds(pl.multiple_of(half * ROWS, ROWS), ROWS)
        guided_ref[rows] = guided[at].astype(BF16)
        next_ref[rows] = (xcols[rows].astype(F32) + sigma_step * guided[at]).astype(BF16)
    for copy in sent:
        copy.wait_send()


def hand_over(guided_ref, next_ref, guided_out, next_out):
    guided_out[...] = guided_ref[...]
    next_out[...] = next_ref[...]


def per_device(latents, w_qkv, w_out, q_gain, k_gain, text_kv, text_lengths, sigmas, step_index, guidance):
    any_space = pl.BlockSpec(memory_space=pl.ANY)
    vmem = pl.BlockSpec(memory_space=pltpu.VMEM)
    smem = pl.BlockSpec(memory_space=pltpu.SMEM)
    out = jax.ShapeDtypeStruct((2 * ROWS, HALF), BF16)
    guided, latents_after = pl.pallas_call(
        step_kernel,
        name="denoising_step",
        out_shape=(out, out),
        in_specs=[any_space] * 4 + [vmem] * 2 + [smem] * 4,
        out_specs=(vmem, vmem),
        scratch_shapes=[
            pltpu.VMEM((UNITS, 2, ROWS, WIDTH), BF16),
            pltpu.VMEM((WIDTH, 3 * OWN), BF16),
            pltpu.VMEM((2 * OWN, HALF), BF16),
            pltpu.VMEM((2, 2, 256, OWN), BF16),
            pltpu.VMEM((2 * ROWS, HALF), BF16),
            pltpu.VMEM((4, UNITS, HEADS, UNIT, HD), BF16),
            pltpu.VMEM((4, UNITS, 2, HEADS, UNIT, HD), BF16),
            pltpu.VMEM((UNITS, HEADS, UNIT, HD), BF16),
            pltpu.VMEM((HEADS, 2, HD, UNITS * UNIT), F32),
            pltpu.VMEM((HEADS, 2, 8, UNITS * UNIT), F32),
            pltpu.VMEM((UNITS, 3, HEADS, HD + STAT, UNIT), BF16),
            pltpu.VMEM((UNITS, 3, HEADS, HD + STAT, UNIT), BF16),
            pltpu.VMEM((UNITS, HEADS, HD, UNIT), F32),
            pltpu.VMEM((UNITS, 8, UNIT), F32),
            pltpu.VMEM((HEADS, HD, QUERIES), F32),
            pltpu.VMEM((HEADS, 8, QUERIES), F32),
            pltpu.VMEM((UNITS, 2, ROWS, OWN), BF16),
            pltpu.VMEM((UNITS, 2, ROWS, 2 * OWN), BF16),
            pltpu.VMEM((2, ROWS, HALF), BF16),
            pltpu.VMEM((2, 2, PART, HALF), BF16),
            pltpu.VMEM((2, 2, ROWS, HALF), BF16),
            pltpu.VMEM((2, 2, ROWS, HALF), BF16),
            pltpu.SemaphoreType.DMA((16,)),
            pltpu.SemaphoreType.DMA((MESSAGES,)),
            pltpu.SemaphoreType.DMA((MESSAGES,)),
        ],
        compiler_params=pltpu.CompilerParams(
            collective_id=0, has_side_effects=True, vmem_limit_bytes=60 * 2**20
        ),
        cost_estimate=pl.CostEstimate(
            flops=12 * 10**9, bytes_accessed=15 * 10**6, transcendentals=14 * 10**6
        ),
    )(
        latents,
        jnp.transpose(w_qkv, (1, 0, 2)),
        w_out,
        text_kv,
        q_gain.reshape(1, HD),
        k_gain.reshape(1, HD),
        text_lengths,
        sigmas,
        step_index,
        guidance,
    )
    return pl.pallas_call(
        hand_over,
        name="hand_over",
        out_shape=(out, out),
        in_specs=[vmem, vmem],
        out_specs=(vmem, vmem),
    )(guided, latents_after)


def solution(mesh):
    placed = (
        P(("blk", "ulysses"), None),
        P(None, None, "ulysses"),
        P("ulysses", None),
        P(),
        P(),
        P(None, None, None, "ulysses"),
        P(),
        P(),
        P(),
        P(),
    )
    return jax.shard_map(
        per_device,
        mesh=mesh,
        in_specs=placed,
        out_specs=(P(("blk", "ulysses"), "cfg"), P(("blk", "ulysses"), "cfg")),
        check_vma=False,
    )
```
